32 devices in a mesh: seq: 8 (over y, x, core), dp: 4 (over z).
Axes of the slice: x: 2, y: 2, z: 4, core: 2. Of those that a mesh axis runs over, the one named last changes fastest.
Arguments:
- coarse: bfloat16 [4, 2048, 768], P('dp', 'seq'), may hold values from -6 to 6
- skip: bfloat16 [4, 4096, 768], P('dp', 'seq'), may hold values from -6 to 6
- skip_weight: bfloat16 [768, 768], P('seq'), may hold values from -0.21875 to 0.21875
- depth_taps: float32 [3, 768], replicated, may hold values from -3 to 3
- cotangent: bfloat16 [4, 4096, 768], P('dp', 'seq'), may hold values from -6 to 6
Outputs:
- grad_coarse: bfloat16 [4, 2048, 768], P('dp', 'seq')
- grad_skip: bfloat16 [4, 4096, 768], P('dp', 'seq')
- grad_skip_weight: float32 [768, 768], P('seq')
- grad_taps: float32 [3, 768], replicated
The draws below stay inside these ranges and needn't reach their ends.
All inputs are finite; a program needn't handle non-finite values.
Results may differ from the reference program's by a relative error of at most 0.006.
Values may be sent and summed in bfloat16 or wider, within the bound.
A program may use at most 64 MiB of HBM per device.

```python
import math
import jax
import jax.numpy as jnp
from jax import lax

CS = 768
LEN = 2048
FINE = 4096
BATCH = 4


def with_spikes(result, own_key, source, target, shards_of, factor):
    owner, partner = [(jnp.arange(result.shape[dim]) // (result.shape[dim] // shards_of)).reshape([-1 if axis == dim else 1 for axis in range(result.ndim)]) for dim in (source, target)]
    chosen = jax.random.permutation(own_key, shards_of)[partner]
    strong = (owner == chosen) | (owner == (partner + shards_of // 2) % shards_of)
    return jnp.where(strong, factor * result, result)


def level_of(key, extent, split, low, top_value):
    def one(position, blocks):
        steps = jax.random.uniform(jax.random.fold_in(jax.random.fold_in(key, 6), position), (blocks,), jnp.float32, low / len(split), top_value / len(split))
        return jnp.repeat(jnp.exp(steps), extent[position] // blocks).reshape((-1,) + (1,) * (len(extent) - position - 1))

    gain = one(*split[0])
    for cut in split[1:]:
        gain = gain * one(*cut)
    return gain


def centred(stream_key, extent, scale, bound, shards=(), dtype=jnp.bfloat16):
    values = jax.random.normal(stream_key, extent, jnp.float32) * scale
    if len(shards) > 0:
        values = level_of(stream_key, extent, shards, -0.22, 0.18) * values
    return jnp.clip(values, min=-bound, max=bound).astype(dtype)


def heavy_noise(own_key, dims, deviation, limit, shards, heavy, kind=jnp.bfloat16):
    values = deviation * jax.random.normal(own_key, dims, jnp.float32)
    if shards:
        values = values * level_of(own_key, dims, shards, -0.22, 0.18)
    return jnp.clip(with_spikes(values, jax.random.fold_in(own_key, 3), *heavy), -limit, limit).astype(kind)


def setup_inputs(seed: int = 0) -> dict:
    key_list = jax.random.split(jax.random.key(seed), 6)
    return {
        "coarse": centred(key_list[0], (BATCH, LEN, CS), 1.0, 6.0, ((0, 4), (1, 8))),
        "skip": heavy_noise(key_list[1], (BATCH, FINE, CS), 1.0, 6.0, ((0, 4), (1, 8)), (1, 2, 8, 2.0)),
        "skip_weight": centred(key_list[2], (CS, CS), CS ** -0.5, 0.21875, ((0, 8),)),
        "depth_taps": centred(key_list[3], (3, CS), 0.5, 3.0, (), jnp.float32),
        "cotangent": centred(key_list[4], (BATCH, FINE, CS), 1.0, 6.0, ((0, 4), (1, 8))),
    }


inv_root_two = 0.7071067811865476
inv_root_tau = 0.3989422804014327

def gelu_slope(pre_act):
    normal_cdf = 0.5 * (1.0 + lax.erf(pre_act * inv_root_two))
    normal_pdf = jnp.exp(-0.5 * pre_act * pre_act) * inv_root_tau
    return normal_cdf + pre_act * normal_pdf

def reference(coarse, skip, skip_weight, depth_taps, cotangent):

    def one_sequence(running, inputs):
        coarse_seq, skip_seq, cotangent_seq = inputs
        projected = jnp.dot(skip_seq, skip_weight, preferred_element_type=jnp.float32)
        upsampled = jnp.repeat(coarse_seq, 2, axis=0).astype(jnp.float32)
        merged = (upsampled + projected).astype(jnp.bfloat16)
        padded = jnp.pad(merged, ((1, 1), (0, 0)))
        pre_act = depth_taps[0] * padded[:-2] + depth_taps[1] * padded[1:-1] + depth_taps[2] * padded[2:]
        grad_pre = (cotangent_seq * gelu_slope(pre_act)).astype(jnp.bfloat16)
        grad_padded = jnp.pad(grad_pre, ((1, 1), (0, 0)))
        grad_merged = (cotangent_seq.astype(jnp.float32) + depth_taps[0] * grad_padded[2:] + depth_taps[1] * grad_padded[1:-1] + depth_taps[2] * grad_padded[:-2]).astype(jnp.bfloat16)
        positions = merged.shape[0]
        tap_terms = jnp.stack([lax.optimization_barrier(jnp.sum(padded[offset:offset + positions].astype(jnp.float32) * grad_pre.astype(jnp.float32), axis=0)) for offset in range(3)])
        weight_term = jnp.dot(skip_seq.T, grad_merged, preferred_element_type=jnp.float32)
        grad_skip_seq = jnp.dot(grad_merged, skip_weight.T, preferred_element_type=jnp.float32).astype(jnp.bfloat16)
        grad_coarse_seq = grad_merged.astype(jnp.float32).reshape(-1, 2, grad_merged.shape[1]).sum(axis=1).astype(jnp.bfloat16)
        return ((running[0] + weight_term, running[1] + tap_terms), (grad_coarse_seq, grad_skip_seq))
    width_all = skip.shape[2]
    start_state = (jnp.zeros((width_all, width_all), jnp.float32), jnp.zeros((3, width_all), jnp.float32))
    (weight_sum, tap_sum), (grad_coarse, grad_skip) = lax.scan(one_sequence, start_state, (coarse, skip, cotangent))
    grad_scale = 1.0 / math.sqrt(BATCH * FINE)
    return (grad_coarse, grad_skip, weight_sum * grad_scale, tap_sum * grad_scale)
```

```python
import functools
import math

import jax
import jax.numpy as jnp
from jax import lax
from jax.experimental import pallas as pl
from jax.experimental.pallas import tpu as pltpu
from jax.sharding import PartitionSpec as P

inv_root_two = 0.7071067811865476
inv_root_tau = 0.3989422804014327


def padded_2(cells, sides, width):
    for axis, dim in sides:
        count = lax.axis_size(axis)
        ends = count - 1
        head = lax.slice_in_dim(cells, 0, width, axis=dim)
        tail = lax.slice_in_dim(cells, cells.shape[dim] - width, cells.shape[dim], axis=dim)
        cells = jnp.concatenate(
            [
                lax.ppermute(tail, axis, [(i, (i + 1) % count) for i in range(ends)]),
                cells,
                lax.ppermute(head, axis, [((i + 1) % count, i) for i in range(ends)]),
            ],
            axis=dim,
        )
    return cells


def gelu_slope(pre_act):
    normal_cdf = 0.5 * (1.0 + lax.erf(pre_act * inv_root_two))
    normal_pdf = jnp.exp(-0.5 * pre_act * pre_act) * inv_root_tau
    return normal_cdf + pre_act * normal_pdf


def local(coarse, skip, skip_weight, depth_taps, cotangent):
    batch_rows, fine_rows, channels = skip.shape
    flat_count = batch_rows * fine_rows
    shard_rows = skip_weight.shape[0]
    flat_skip = skip.reshape(flat_count, channels)
    full_weight = lax.all_gather(skip_weight, "seq", axis=0, tiled=True)
    projected = jnp.dot(flat_skip, full_weight, preferred_element_type=jnp.float32)
    upsampled = jnp.broadcast_to(
        coarse[:, :, None, :], (batch_rows, fine_rows // 2, 2, channels)
    ).reshape(flat_count, channels)
    merged = (
        (upsampled.astype(jnp.float32) + projected)
        .astype(jnp.bfloat16)
        .reshape(batch_rows, fine_rows, channels)
    )
    padded = padded_2(merged, (("seq", 1),), 1)
    pre_act = (
        depth_taps[0] * padded[:, :-2]
        + depth_taps[1] * padded[:, 1:-1]
        + depth_taps[2] * padded[:, 2:]
    )
    grad_pre = (cotangent * gelu_slope(pre_act)).astype(jnp.bfloat16)
    grad_padded = padded_2(grad_pre, (("seq", 1),), 1)
    grad_merged = (
        cotangent.astype(jnp.float32)
        + depth_taps[0] * grad_padded[:, 2:]
        + depth_taps[1] * grad_padded[:, 1:-1]
        + depth_taps[2] * grad_padded[:, :-2]
    ).astype(jnp.bfloat16)
    flat_grad = grad_merged.reshape(flat_count, channels)
    grad_wide = grad_pre.astype(jnp.float32)
    tap_terms = jnp.stack(
        [
            jnp.sum(
                padded[:, offset : offset + fine_rows].astype(jnp.float32) * grad_wide, axis=(0, 1)
            )
            for offset in range(3)
        ]
    )
    grad_scale = 1.0 / math.sqrt(flat_count * lax.axis_size("seq") * lax.axis_size("dp"))
    summed, tap_sum = lax.psum(
        (
            lax.dot_general(
                flat_skip, flat_grad, (((0,), (0,)), ((), ())), preferred_element_type=jnp.float32
            ),
            tap_terms,
        ),
        ("seq", "dp"),
    )
    weight_sum = lax.dynamic_slice_in_dim(summed, lax.axis_index("seq") * shard_rows, shard_rows, 0)
    grad_skip = lax.dot_general(
        flat_grad, full_weight, (((1,), (1,)), ((), ())), preferred_element_type=jnp.float32
    )
    grad_coarse = (
        grad_merged.astype(jnp.float32)
        .reshape(batch_rows, fine_rows // 2, 2, channels)
        .sum(axis=2)
        .astype(jnp.bfloat16)
    )
    grad_skip = grad_skip.astype(jnp.bfloat16).reshape(batch_rows, fine_rows, channels)
    return (grad_coarse, grad_skip, weight_sum * grad_scale, tap_sum * grad_scale)


MESH = pl.DeviceIdType.MESH
halo = 16
tile = 64
width = 256


def send(src, dst, send_sem, recv_sem, axis, target):
    return pltpu.make_async_remote_copy(
        src_ref=src,
        dst_ref=dst,
        send_sem=send_sem,
        recv_sem=recv_sem,
        device_id={axis: target},
        device_id_type=MESH,
    )


def kernel(
    seq_count,
    dp_count,
    grad_scale,
    coarse_hbm,
    skip_hbm,
    weight_ref,
    taps_ref,
    cot_hbm,
    coarse_out,
    skip_out,
    weight_out,
    taps_out,
    skip_ext,
    cot_ext,
    coarse_ext,
    skip_turned,
    repeat_mat,
    pair_mat,
    weights,
    merged,
    grad_pre,
    grad_merged,
    coarse_grad,
    skip_grad,
    term_wide,
    term_half,
    from_core,
    chip_half,
    chip_own,
    from_chips,
    plane_wide,
    plane_half,
    from_planes,
    final,
    tap_own,
    tap_core,
    tap_chips,
    tap_planes,
    local_sem,
    halo_send,
    halo_recv,
    gather_send,
    gather_recv,
    forward_send,
    forward_recv,
    sib_send,
    sib_recv,
    core_send,
    core_recv,
    chip_send,
    chip_recv,
    plane_send,
    plane_recv,
    final_send,
    final_recv,
    tap_send,
    tap_recv,
):
    rows = skip_hbm.shape[1]
    channels = skip_hbm.shape[2]
    shard = weight_ref.shape[0]
    chunks = channels // width
    chips = seq_count // 2
    me = lax.axis_index("seq")
    plane = lax.axis_index("dp")
    core = lax.rem(me, 2)
    chip = lax.div(me, 2)
    sibling = me + 1 - 2 * core
    right = lax.rem(me + 1, seq_count)
    left = lax.rem(me + seq_count - 1, seq_count)

    loads = [
        pltpu.make_async_copy(skip_hbm.at[0], skip_ext.at[pl.ds(halo, rows)], local_sem.at[0]),
        pltpu.make_async_copy(cot_hbm.at[0], cot_ext.at[pl.ds(halo, rows)], local_sem.at[1]),
        pltpu.make_async_copy(
            coarse_hbm.at[0], coarse_ext.at[pl.ds(halo, rows // 2)], local_sem.at[2]
        ),
    ]
    for copy in loads:
        copy.start()

    barrier = pltpu.get_barrier_semaphore()
    for step in range(1, seq_count):
        pl.semaphore_signal(
            barrier, inc=1, device_id={"seq": lax.rem(me + step, seq_count)}, device_id_type=MESH
        )
    for step in range(1, dp_count):
        pl.semaphore_signal(
            barrier, inc=1, device_id={"dp": lax.rem(plane + step, dp_count)}, device_id_type=MESH
        )
    pl.semaphore_wait(barrier, seq_count + dp_count - 2)

    sends = []

    def launch(copy):
        copy.start()
        sends.append(copy)
        return copy

    def cols(chunk):
        return pl.ds(chunk * width, width)

    gathers, own_halves = {}, {}

    def gather(chunk):
        for step in range(1, chips):
            target = 2 * lax.rem(chip + step, chips) + core
            gathers[chunk, step] = launch(
                send(
                    weight_ref.at[:, cols(chunk)],
                    weights.at[chunk, me],
                    gather_send.at[chunk, step - 1],
                    gather_recv.at[chunk, step - 1],
                    "seq",
                    target,
                )
            )
        own_halves[chunk] = launch(
            send(
                weight_ref.at[:, cols(chunk)],
                weights.at[chunk, me],
                sib_send.at[chunk],
                sib_recv.at[chunk],
                "seq",
                sibling,
            )
        )

    gather(0)
    halos = []
    pairs = ((skip_hbm, skip_ext, rows), (coarse_hbm, coarse_ext, rows // 2), (cot_hbm, cot_ext, rows))
    for number, (source, target, count) in enumerate(pairs):
        halos.append(
            launch(
                send(
                    source.at[0, pl.ds(count - halo, halo)],
                    target.at[pl.ds(0, halo)],
                    halo_send.at[2 * number],
                    halo_recv.at[2 * number],
                    "seq",
                    right,
                )
            )
        )
        halos.append(
            launch(
                send(
                    source.at[0, pl.ds(0, halo)],
                    target.at[pl.ds(count + halo, halo)],
                    halo_send.at[2 * number + 1],
                    halo_recv.at[2 * number + 1],
                    "seq",
                    left,
                )
            )
        )
    for chunk in range(1, chunks):
        gather(chunk)

    for chunk in range(chunks):
        weights[chunk, me] = weight_ref[:, cols(chunk)]
    out_row = lax.broadcasted_iota(jnp.int32, repeat_mat.shape, 0)
    in_row = lax.broadcasted_iota(jnp.int32, repeat_mat.shape, 1)
    repeat_mat[...] = jnp.where(
        lax.shift_right_logical(out_row, 1) + halo // 2 == in_row, 1.0, 0.0
    ).astype(jnp.bfloat16)
    out_row = lax.broadcasted_iota(jnp.int32, pair_mat.shape, 0)
    in_row = lax.broadcasted_iota(jnp.int32, pair_mat.shape, 1)
    pair_mat[...] = jnp.where(lax.shift_right_logical(in_row, 1) == out_row, 1.0, 0.0).astype(
        jnp.bfloat16
    )
    tap_own[...] = jnp.zeros_like(tap_own)
    for copy in loads:
        copy.wait()
    skip_turned[...] = skip_ext[pl.ds(halo, rows), :].T

    low_in = jnp.where(me == 0, 0.0, 1.0)
    high_in = jnp.where(me == seq_count - 1, 0.0, 1.0)
    forwards = {}

    def forward(chunk):
        for step in range(1, chips):
            gathers[chunk, step].wait_recv()
            owner = 2 * lax.rem(chip + chips - step, chips) + core
            forwards[chunk, step] = launch(
                send(
                    weights.at[chunk, owner],
                    weights.at[chunk, owner],
                    forward_send.at[chunk, step - 1],
                    forward_recv.at[chunk, step - 1],
                    "seq",
                    sibling,
                )
            )

    def project(chunk):
        own_halves[chunk].wait_recv()
        for step in range(1, chips):
            forwards[chunk, step].wait_recv()
        dense = weights[chunk].reshape(channels, width)
        values = jnp.dot(skip_ext[...], dense, preferred_element_type=jnp.float32) + jnp.dot(
            repeat_mat[...], coarse_ext[:, cols(chunk)], preferred_element_type=jnp.float32
        )
        values = values.astype(jnp.bfloat16).astype(jnp.float32)
        merged[pl.ds(0, halo), :] = values[:halo] * low_in
        merged[pl.ds(halo, rows), :] = values[halo : halo + rows]
        merged[pl.ds(halo + rows, halo), :] = values[halo + rows :] * high_in

    def slopes(chunk):
        tap = [taps_ref[pl.ds(k, 1), cols(chunk)] for k in range(3)]

        def one(first, count, cot):
            near = [merged[pl.ds(first + k - 1, count), :] for k in range(3)]
            pre_act = tap[0] * near[0] + tap[1] * near[1] + tap[2] * near[2]
            return near, (cot * gelu_slope(pre_act)).astype(jnp.bfloat16).astype(jnp.float32)

        edge = cot_ext[pl.ds(0, halo), cols(chunk)].astype(jnp.float32)
        grad_pre[pl.ds(8, 8), :] = one(8, 8, edge[8:])[1] * low_in
        edge = cot_ext[pl.ds(halo + rows, halo), cols(chunk)].astype(jnp.float32)
        grad_pre[pl.ds(halo + rows, 8), :] = one(halo + rows, 8, edge[:8])[1] * high_in

        def body(number, totals):
            first = halo + number * tile
            cot = cot_ext[pl.ds(first, tile), cols(chunk)].astype(jnp.float32)
            near, grad = one(first, tile, cot)
            grad_pre[pl.ds(first, tile), :] = grad
            return tuple(
                total + jnp.sum((part * grad).reshape(tile // 8, 8, width), axis=0)
                for total, part in zip(totals, near)
            )

        zero = jnp.zeros((8, width), jnp.float32)
        totals = (zero, zero, zero)
        for number in range(rows // tile):
            totals = body(number, totals)
        for k in range(3):
            tap_own[pl.ds(k, 1), cols(chunk)] = jnp.sum(totals[k], axis=0, keepdims=True)

    def back(chunk):
        tap = [taps_ref[pl.ds(k, 1), cols(chunk)] for k in range(3)]

        for number in range(rows // tile):
            first = halo + number * tile
            cot = cot_ext[pl.ds(first, tile), cols(chunk)].astype(jnp.float32)
            grad_merged[pl.ds(first - halo, tile), cols(chunk)] = (
                cot
                + tap[0] * grad_pre[pl.ds(first + 1, tile), :]
                + tap[1] * grad_pre[pl.ds(first, tile), :]
                + tap[2] * grad_pre[pl.ds(first - 1, tile), :]
            ).astype(jnp.bfloat16)

    core_copies, chip_copies, plane_copies, final_copies = {}, {}, {}, {}

    def weight_terms(chunk):
        terms = jnp.dot(
            skip_turned[...], grad_merged[:, cols(chunk)], preferred_element_type=jnp.float32
        )
        for block in range(seq_count):
            part = terms[block * shard : (block + 1) * shard]
            term_wide[chunk, block % 2, block // 2] = part
            term_half[chunk, block % 2, block // 2] = part.astype(jnp.bfloat16)
        core_copies[chunk] = launch(
            send(
                term_half.at[chunk, 1 - core],
                from_core.at[chunk],
                core_send.at[chunk],
                core_recv.at[chunk],
                "seq",
                sibling,
            )
        )

    def over_chips(chunk):
        core_copies[chunk].wait_recv()
        for block in range(chips):
            chip_half[chunk, block] = (
                term_wide[chunk, core, block] + from_core[chunk, block].astype(jnp.float32)
            ).astype(jnp.bfloat16)
        for step in range(1, chips):
            target = lax.rem(chip + step, chips)
            chip_copies[chunk, step] = launch(
                send(
                    chip_half.at[chunk, target],
                    from_chips.at[chunk, step - 1],
                    chip_send.at[chunk, step - 1],
                    chip_recv.at[chunk, step - 1],
                    "seq",
                    2 * target + core,
                )
            )
        chip_own[chunk] = term_wide[chunk, core, chip] + from_core[chunk, chip].astype(jnp.float32)

    def over_planes(chunk):
        total = chip_own[chunk]
        for step in range(1, chips):
            chip_copies[chunk, step].wait_recv()
            total = total + from_chips[chunk, step - 1].astype(jnp.float32)
        for part in range(4):
            piece = total[
                (part // 2) * (shard // 2) : (part // 2 + 1) * (shard // 2),
                (part % 2) * 128 : (part % 2 + 1) * 128,
            ]
            plane_wide[chunk, part] = piece
            plane_half[chunk, part] = piece.astype(jnp.bfloat16)
        for step in range(1, dp_count):
            target = lax.rem(plane + step, dp_count)
            plane_copies[chunk, step] = launch(
                send(
                    plane_half.at[chunk, target],
                    from_planes.at[chunk, step - 1],
                    plane_send.at[chunk, step - 1],
                    plane_recv.at[chunk, step - 1],
                    "dp",
                    target,
                )
            )

    def spread(chunk):
        total = plane_wide[chunk, plane]
        for step in range(1, dp_count):
            plane_copies[chunk, step].wait_recv()
            total = total + from_planes[chunk, step - 1].astype(jnp.float32)
        final[chunk, plane] = total.astype(jnp.bfloat16)
        for step in range(1, dp_count):
            target = lax.rem(plane + step, dp_count)
            final_copies[chunk, step] = launch(
                send(
                    final.at[chunk, plane],
                    final.at[chunk, plane],
                    final_send.at[chunk, step - 1],
                    final_recv.at[chunk, step - 1],
                    "dp",
                    target,
                )
            )

    def finish(chunk):
        for step in range(1, dp_count):
            final_copies[chunk, step].wait_recv()
        for part in range(4):
            weight_out[
                pl.ds((part // 2) * (shard // 2), shard // 2),
                pl.ds(chunk * width + (part % 2) * 128, 128),
            ] = final[chunk, part].astype(jnp.float32) * grad_scale

    forward(0)
    for copy in halos:
        copy.wait_recv()
    for chunk in range(chunks):
        project(chunk)
        if chunk + 1 < chunks:
            forward(chunk + 1)
        if chunk >= 2:
            spread(chunk - 2)
        if chunk >= 1:
            over_chips(chunk - 1)
        slopes(chunk)
        if chunk == chunks - 1:
            tap_pair = launch(
                send(tap_own, tap_core, tap_send.at[0], tap_recv.at[0], "seq", sibling)
            )
        if chunk >= 1:
            over_planes(chunk - 1)
        back(chunk)
        weight_terms(chunk)

    last = chunks - 1
    spread(last - 1)
    tap_pair.wait_recv()
    tap_chips[chip] = tap_own[...] + tap_core[...]
    tap_row = []
    for step in range(1, chips):
        tap_row.append(
            launch(
                send(
                    tap_chips.at[chip],
                    tap_chips.at[chip],
                    tap_send.at[step],
                    tap_recv.at[step],
                    "seq",
                    2 * lax.rem(chip + step, chips) + core,
                )
            )
        )
    over_chips(last)
    coarse_grad[...] = jnp.dot(
        pair_mat[...], grad_merged[...], preferred_element_type=jnp.float32
    ).astype(jnp.bfloat16)
    store_coarse = pltpu.make_async_copy(coarse_grad, coarse_out.at[0], local_sem.at[3])
    store_coarse.start()
    for copy in tap_row:
        copy.wait_recv()
    total = tap_chips[0]
    for block in range(1, chips):
        total = total + tap_chips[block]
    tap_planes[plane] = total
    tap_line = []
    for step in range(1, dp_count):
        tap_line.append(
            launch(
                send(
                    tap_planes.at[plane],
                    tap_planes.at[plane],
                    tap_send.at[chips - 1 + step],
                    tap_recv.at[chips - 1 + step],
                    "dp",
                    lax.rem(plane + step, dp_count),
                )
            )
        )
    over_planes(last)
    values = jnp.zeros((rows, channels), jnp.float32)
    for chunk in range(chunks):
        values = values + lax.dot_general(
            grad_merged[:, cols(chunk)],
            weights[chunk].reshape(channels, width),
            (((1,), (1,)), ((), ())),
            preferred_element_type=jnp.float32,
        )
    skip_grad[...] = values.astype(jnp.bfloat16)
    store_skip = pltpu.make_async_copy(skip_grad, skip_out.at[0], local_sem.at[4])
    store_skip.start()
    for copy in tap_line:
        copy.wait_recv()
    total = tap_planes[0]
    for block in range(1, dp_count):
        total = total + tap_planes[block]
    taps_out[...] = total[:3] * grad_scale
    for chunk in range(last):
        finish(chunk)
    spread(last)
    finish(last)
    store_coarse.wait()
    store_skip.wait()
    for copy in sends:
        copy.wait_send()


def fused(seq_count, dp_count, coarse, skip, skip_weight, depth_taps, cotangent):
    _, rows, channels = skip.shape
    shard = skip_weight.shape[0]
    chunks = channels // width
    chips = seq_count // 2
    half, wide = jnp.bfloat16, jnp.float32
    dma = pltpu.SemaphoreType.DMA
    extended = rows + 2 * halo
    return pl.pallas_call(
        functools.partial(
            kernel, seq_count, dp_count, 1.0 / math.sqrt(rows * seq_count * dp_count)
        ),
        out_shape=(
            jax.ShapeDtypeStruct(coarse.shape, half),
            jax.ShapeDtypeStruct(skip.shape, half),
            jax.ShapeDtypeStruct(skip_weight.shape, wide),
            jax.ShapeDtypeStruct(depth_taps.shape, wide),
        ),
        in_specs=[
            pl.BlockSpec(memory_space=pl.ANY),
            pl.BlockSpec(memory_space=pl.ANY),
            pl.BlockSpec(memory_space=pltpu.VMEM),
            pl.BlockSpec(memory_space=pltpu.VMEM),
            pl.BlockSpec(memory_space=pl.ANY),
        ],
        out_specs=(
            pl.BlockSpec(memory_space=pl.ANY),
            pl.BlockSpec(memory_space=pl.ANY),
            pl.BlockSpec(memory_space=pltpu.VMEM),
            pl.BlockSpec(memory_space=pltpu.VMEM),
        ),
        scratch_shapes=[
            pltpu.VMEM((extended, channels), half),
            pltpu.VMEM((extended, channels), half),
            pltpu.VMEM((rows // 2 + 2 * halo, channels), half),
            pltpu.VMEM((channels, rows), half),
            pltpu.VMEM((extended, rows // 2 + 2 * halo), half),
            pltpu.VMEM((rows // 2, rows), half),
            pltpu.VMEM((chunks, seq_count, shard, width), half),
            pltpu.VMEM((extended, width), wide),
            pltpu.VMEM((extended, width), wide),
            pltpu.VMEM((rows, channels), half),
            pltpu.VMEM((rows // 2, channels), half),
            pltpu.VMEM((rows, channels), half),
            pltpu.VMEM((chunks, 2, chips, shard, width), wide),
            pltpu.VMEM((chunks, 2, chips, shard, width), half),
            pltpu.VMEM((chunks, chips, shard, width), half),
            pltpu.VMEM((chunks, chips, shard, width), half),
            pltpu.VMEM((chunks, shard, width), wide),
            pltpu.VMEM((chunks, chips - 1, shard, width), half),
            pltpu.VMEM((chunks, 4, shard // 2, 128), wide),
            pltpu.VMEM((chunks, 4, shard // 2, 128), half),
            pltpu.VMEM((chunks, dp_count - 1, shard // 2, 128), half),
            pltpu.VMEM((chunks, 4, shard // 2, 128), half),
            pltpu.VMEM((8, channels), wide),
            pltpu.VMEM((8, channels), wide),
            pltpu.VMEM((chips, 8, channels), wide),
            pltpu.VMEM((dp_count, 8, channels), wide),
            dma((5,)),
            dma((6,)),
            dma((6,)),
            dma((chunks, chips - 1)),
            dma((chunks, chips - 1)),
            dma((chunks, chips - 1)),
            dma((chunks, chips - 1)),
            dma((chunks,)),
            dma((chunks,)),
            dma((chunks,)),
            dma((chunks,)),
            dma((chunks, chips - 1)),
            dma((chunks, chips - 1)),
            dma((chunks, dp_count - 1)),
            dma((chunks, dp_count - 1)),
            dma((chunks, dp_count - 1)),
            dma((chunks, dp_count - 1)),
            dma((chips + dp_count - 1,)),
            dma((chips + dp_count - 1,)),
        ],
        compiler_params=pltpu.CompilerParams(
            collective_id=0, has_side_effects=True, vmem_limit_bytes=48 * 1024 * 1024
        ),
    )(coarse, skip, skip_weight, depth_taps, cotangent)


def solution(mesh):
    placed = (P("dp", "seq", None), P("dp", "seq", None), P("seq", None), P(), P("dp", "seq", None))
    seq_count, dp_count = mesh.shape["seq"], mesh.shape["dp"]

    def device_part(coarse, skip, skip_weight, depth_taps, cotangent):
        fits = (
            skip.shape[0] == 1
            and skip.shape[1] % tile == 0
            and skip.shape[2] % width == 0
            and skip_weight.shape[0] % 32 == 0
            and seq_count % 2 == 0
            and seq_count > 2
            and dp_count == 4
        )
        if fits:
            return fused(seq_count, dp_count, coarse, skip, skip_weight, depth_taps, cotangent)
        return local(coarse, skip, skip_weight, depth_taps, cotangent)

    return jax.shard_map(
        device_part,
        mesh=mesh,
        in_specs=placed,
        out_specs=(P("dp", "seq", None), P("dp", "seq", None), P("seq", None), P()),
        check_vma=False,
    )
```

```python
import functools
import math

import jax
import jax.numpy as jnp
from jax import lax
from jax.experimental import pallas as pl
from jax.experimental.pallas import tpu as pltpu
from jax.sharding import PartitionSpec as P

inv_root_two = 0.7071067811865476
inv_root_tau = 0.3989422804014327


def padded_2(cells, sides, width):
    for axis, dim in sides:
        count = lax.axis_size(axis)
        ends = count - 1
        head = lax.slice_in_dim(cells, 0, width, axis=dim)
        tail = lax.slice_in_dim(cells, cells.shape[dim] - width, cells.shape[dim], axis=dim)
        cells = jnp.concatenate(
            [
                lax.ppermute(tail, axis, [(i, (i + 1) % count) for i in range(ends)]),
                cells,
                lax.ppermute(head, axis, [((i + 1) % count, i) for i in range(ends)]),
            ],
            axis=dim,
        )
    return cells


def gelu_slope(pre_act):
    normal_cdf = 0.5 * (1.0 + lax.erf(pre_act * inv_root_two))
    normal_pdf = jnp.exp(-0.5 * pre_act * pre_act) * inv_root_tau
    return normal_cdf + pre_act * normal_pdf


def local(coarse, skip, skip_weight, depth_taps, cotangent):
    batch_rows, fine_rows, channels = skip.shape
    flat_count = batch_rows * fine_rows
    shard_rows = skip_weight.shape[0]
    flat_skip = skip.reshape(flat_count, channels)
    full_weight = lax.all_gather(skip_weight, "seq", axis=0, tiled=True)
    projected = jnp.dot(flat_skip, full_weight, preferred_element_type=jnp.float32)
    upsampled = jnp.broadcast_to(
        coarse[:, :, None, :], (batch_rows, fine_rows // 2, 2, channels)
    ).reshape(flat_count, channels)
    merged = (
        (upsampled.astype(jnp.float32) + projected)
        .astype(jnp.bfloat16)
        .reshape(batch_rows, fine_rows, channels)
    )
    padded = padded_2(merged, (("seq", 1),), 1)
    pre_act = (
        depth_taps[0] * padded[:, :-2]
        + depth_taps[1] * padded[:, 1:-1]
        + depth_taps[2] * padded[:, 2:]
    )
    grad_pre = (cotangent * gelu_slope(pre_act)).astype(jnp.bfloat16)
    grad_padded = padded_2(grad_pre, (("seq", 1),), 1)
    grad_merged = (
        cotangent.astype(jnp.float32)
        + depth_taps[0] * grad_padded[:, 2:]
        + depth_taps[1] * grad_padded[:, 1:-1]
        + depth_taps[2] * grad_padded[:, :-2]
    ).astype(jnp.bfloat16)
    flat_grad = grad_merged.reshape(flat_count, channels)
    grad_wide = grad_pre.astype(jnp.float32)
    tap_terms = jnp.stack(
        [
            jnp.sum(
                padded[:, offset : offset + fine_rows].astype(jnp.float32) * grad_wide, axis=(0, 1)
            )
            for offset in range(3)
        ]
    )
    grad_scale = 1.0 / math.sqrt(flat_count * lax.axis_size("seq") * lax.axis_size("dp"))
    summed, tap_sum = lax.psum(
        (
            lax.dot_general(
                flat_skip, flat_grad, (((0,), (0,)), ((), ())), preferred_element_type=jnp.float32
            ),
            tap_terms,
        ),
        ("seq", "dp"),
    )
    weight_sum = lax.dynamic_slice_in_dim(summed, lax.axis_index("seq") * shard_rows, shard_rows, 0)
    grad_skip = lax.dot_general(
        flat_grad, full_weight, (((1,), (1,)), ((), ())), preferred_element_type=jnp.float32
    )
    grad_coarse = (
        grad_merged.astype(jnp.float32)
        .reshape(batch_rows, fine_rows // 2, 2, channels)
        .sum(axis=2)
        .astype(jnp.bfloat16)
    )
    grad_skip = grad_skip.astype(jnp.bfloat16).reshape(batch_rows, fine_rows, channels)
    return (grad_coarse, grad_skip, weight_sum * grad_scale, tap_sum * grad_scale)


MESH = pl.DeviceIdType.MESH
halo = 16
tile = 64
width = 256


def send(src, dst, send_sem, recv_sem, axis, target):
    return pltpu.make_async_remote_copy(
        src_ref=src,
        dst_ref=dst,
        send_sem=send_sem,
        recv_sem=recv_sem,
        device_id={axis: target},
        device_id_type=MESH,
    )


def kernel(
    seq_count,
    dp_count,
    grad_scale,
    coarse_hbm,
    skip_hbm,
    weight_hbm,
    taps_hbm,
    cot_hbm,
    coarse_hbm_out,
    skip_hbm_out,
    weight_hbm_out,
    taps_hbm_out,
    coarse_out,
    skip_out,
    weight_out,
    taps_out,
    skip_ext,
    cot_ext,
    coarse_ext,
    skip_turned,
    repeat_mat,
    pair_mat,
    weights,
    merged,
    grad_pre,
    grad_merged,
    term_wide,
    term_half,
    from_core,
    chip_half,
    chip_own,
    from_chips,
    plane_wide,
    plane_half,
    from_planes,
    final,
    taps_ref,
    tap_own,
    tap_core,
    tap_chips,
    tap_planes,
    local_sem,
    halo_send,
    halo_recv,
    gather_send,
    gather_recv,
    forward_send,
    forward_recv,
    sib_send,
    sib_recv,
    core_send,
    core_recv,
    chip_send,
    chip_recv,
    plane_send,
    plane_recv,
    final_send,
    final_recv,
    tap_send,
    tap_recv,
):
    rows = skip_hbm.shape[1]
    channels = skip_hbm.shape[2]
    shard = weight_hbm.shape[0]
    chunks = channels // width
    chips = seq_count // 2
    me = lax.axis_index("seq")
    plane = lax.axis_index("dp")
    core = lax.rem(me, 2)
    chip = lax.div(me, 2)
    sibling = me + 1 - 2 * core
    right = lax.rem(me + 1, seq_count)
    left = lax.rem(me + seq_count - 1, seq_count)

    loads = [
        pltpu.make_async_copy(skip_hbm.at[0], skip_ext.at[pl.ds(halo, rows)], local_sem.at[0]),
        pltpu.make_async_copy(cot_hbm.at[0], cot_ext.at[pl.ds(halo, rows)], local_sem.at[1]),
        pltpu.make_async_copy(
            coarse_hbm.at[0], coarse_ext.at[pl.ds(halo, rows // 2)], local_sem.at[2]
        ),
    ]
    loads.append(pltpu.make_async_copy(taps_hbm, taps_ref, local_sem.at[3]))
    for chunk in range(channels // width):
        loads.append(
            pltpu.make_async_copy(
                weight_hbm.at[:, pl.ds(chunk * width, width)],
                weights.at[chunk, me],
                local_sem.at[4 + chunk],
            )
        )
    for copy in loads:
        copy.start()

    barrier = pltpu.get_barrier_semaphore()
    for step in range(1, seq_count):
        pl.semaphore_signal(
            barrier, inc=1, device_id={"seq": lax.rem(me + step, seq_count)}, device_id_type=MESH
        )
    for step in range(1, dp_count):
        pl.semaphore_signal(
            barrier, inc=1, device_id={"dp": lax.rem(plane + step, dp_count)}, device_id_type=MESH
        )
    pl.semaphore_wait(barrier, seq_count + dp_count - 2)

    sends = []
    stores = []

    def write(source, target, number):
        stores.append(
            pltpu.make_async_copy(source, target, local_sem.at[4 + channels // width + number])
        )
        stores[-1].start()


    def launch(copy):
        copy.start()
        sends.append(copy)
        return copy

    def cols(chunk):
        return pl.ds(chunk * width, width)

    gathers, own_halves = {}, {}

    def gather(chunk):
        for step in range(1, chips):
            target = 2 * lax.rem(chip + step, chips) + core
            gathers[chunk, step] = launch(
                send(
                    weight_hbm.at[:, cols(chunk)],
                    weights.at[chunk, me],
                    gather_send.at[chunk, step - 1],
                    gather_recv.at[chunk, step - 1],
                    "seq",
                    target,
                )
            )
        own_halves[chunk] = launch(
            send(
                weight_hbm.at[:, cols(chunk)],
                weights.at[chunk, me],
                sib_send.at[chunk],
                sib_recv.at[chunk],
                "seq",
                sibling,
            )
        )

    gather(0)
    halos = []
    pairs = ((skip_hbm, skip_ext, rows), (coarse_hbm, coarse_ext, rows // 2), (cot_hbm, cot_ext, rows))
    for number, (source, target, count) in enumerate(pairs):
        halos.append(
            launch(
                send(
                    source.at[0, pl.ds(count - halo, halo)],
                    target.at[pl.ds(0, halo)],
                    halo_send.at[2 * number],
                    halo_recv.at[2 * number],
                    "seq",
                    right,
                )
            )
        )
        halos.append(
            launch(
                send(
                    source.at[0, pl.ds(0, halo)],
                    target.at[pl.ds(count + halo, halo)],
                    halo_send.at[2 * number + 1],
                    halo_recv.at[2 * number + 1],
                    "seq",
                    left,
                )
            )
        )
    for chunk in range(1, chunks):
        gather(chunk)

    out_row = lax.broadcasted_iota(jnp.int32, repeat_mat.shape, 0)
    in_row = lax.broadcasted_iota(jnp.int32, repeat_mat.shape, 1)
    repeat_mat[...] = jnp.where(
        lax.shift_right_logical(out_row, 1) + halo // 2 == in_row, 1.0, 0.0
    ).astype(jnp.bfloat16)
    out_row = lax.broadcasted_iota(jnp.int32, pair_mat.shape, 0)
    in_row = lax.broadcasted_iota(jnp.int32, pair_mat.shape, 1)
    pair_mat[...] = jnp.where(lax.shift_right_logical(in_row, 1) == out_row, 1.0, 0.0).astype(
        jnp.bfloat16
    )
    tap_own[...] = jnp.zeros_like(tap_own)
    for copy in loads:
        copy.wait()
    skip_turned[...] = skip_ext[pl.ds(halo, rows), :].T

    low_in = jnp.where(me == 0, 0.0, 1.0)
    high_in = jnp.where(me == seq_count - 1, 0.0, 1.0)
    forwards = {}

    def forward(chunk):
        for step in range(1, chips):
            gathers[chunk, step].wait_recv()
            owner = 2 * lax.rem(chip + chips - step, chips) + core
            forwards[chunk, step] = launch(
                send(
                    weights.at[chunk, owner],
                    weights.at[chunk, owner],
                    forward_send.at[chunk, step - 1],
                    forward_recv.at[chunk, step - 1],
                    "seq",
                    sibling,
                )
            )

    def project(chunk):
        own_halves[chunk].wait_recv()
        for step in range(1, chips):
            forwards[chunk, step].wait_recv()
        dense = weights[chunk].reshape(channels, width)
        values = jnp.dot(skip_ext[...], dense, preferred_element_type=jnp.float32) + jnp.dot(
            repeat_mat[...], coarse_ext[:, cols(chunk)], preferred_element_type=jnp.float32
        )
        values = values.astype(jnp.bfloat16).astype(jnp.float32)
        merged[pl.ds(0, halo), :] = values[:halo] * low_in
        merged[pl.ds(halo, rows), :] = values[halo : halo + rows]
        merged[pl.ds(halo + rows, halo), :] = values[halo + rows :] * high_in

    def slopes(chunk):
        tap = [taps_ref[pl.ds(k, 1), cols(chunk)] for k in range(3)]

        def one(first, count, cot):
            near = [merged[pl.ds(first + k - 1, count), :] for k in range(3)]
            pre_act = tap[0] * near[0] + tap[1] * near[1] + tap[2] * near[2]
            return near, (cot * gelu_slope(pre_act)).astype(jnp.bfloat16).astype(jnp.float32)

        edge = cot_ext[pl.ds(0, halo), cols(chunk)].astype(jnp.float32)
        grad_pre[pl.ds(8, 8), :] = one(8, 8, edge[8:])[1] * low_in
        edge = cot_ext[pl.ds(halo + rows, halo), cols(chunk)].astype(jnp.float32)
        grad_pre[pl.ds(halo + rows, 8), :] = one(halo + rows, 8, edge[:8])[1] * high_in

        def body(number, totals):
            first = halo + number * tile
            cot = cot_ext[pl.ds(first, tile), cols(chunk)].astype(jnp.float32)
            near, grad = one(first, tile, cot)
            grad_pre[pl.ds(first, tile), :] = grad
            return tuple(
                total + jnp.sum((part * grad).reshape(tile // 8, 8, width), axis=0)
                for total, part in zip(totals, near)
            )

        zero = jnp.zeros((8, width), jnp.float32)
        totals = (zero, zero, zero)
        for number in range(rows // tile):
            totals = body(number, totals)
        for k in range(3):
            tap_own[pl.ds(k, 1), cols(chunk)] = jnp.sum(totals[k], axis=0, keepdims=True)

    def back(chunk):
        tap = [taps_ref[pl.ds(k, 1), cols(chunk)] for k in range(3)]

        for number in range(rows // tile):
            first = halo + number * tile
            cot = cot_ext[pl.ds(first, tile), cols(chunk)].astype(jnp.float32)
            grad_merged[pl.ds(first - halo, tile), cols(chunk)] = (
                cot
                + tap[0] * grad_pre[pl.ds(first + 1, tile), :]
                + tap[1] * grad_pre[pl.ds(first, tile), :]
                + tap[2] * grad_pre[pl.ds(first - 1, tile), :]
            ).astype(jnp.bfloat16)

    core_copies, chip_copies, plane_copies, final_copies = {}, {}, {}, {}

    def weight_terms(chunk):
        terms = jnp.dot(
            skip_turned[...], grad_merged[:, cols(chunk)], preferred_element_type=jnp.float32
        )
        for block in range(seq_count):
            part = terms[block * shard : (block + 1) * shard]
            term_wide[chunk, block % 2, block // 2] = part
            term_half[chunk, block % 2, block // 2] = part.astype(jnp.bfloat16)
        core_copies[chunk] = launch(
            send(
                term_half.at[chunk, 1 - core],
                from_core.at[chunk],
                core_send.at[chunk],
                core_recv.at[chunk],
                "seq",
                sibling,
            )
        )

    def over_chips(chunk):
        core_copies[chunk].wait_recv()
        for block in range(chips):
            chip_half[chunk, block] = (
                term_wide[chunk, core, block] + from_core[chunk, block].astype(jnp.float32)
            ).astype(jnp.bfloat16)
        for step in range(1, chips):
            target = lax.rem(chip + step, chips)
            chip_copies[chunk, step] = launch(
                send(
                    chip_half.at[chunk, target],
                    from_chips.at[chunk, step - 1],
                    chip_send.at[chunk, step - 1],
                    chip_recv.at[chunk, step - 1],
                    "seq",
                    2 * target + core,
                )
            )
        chip_own[chunk] = term_wide[chunk, core, chip] + from_core[chunk, chip].astype(jnp.float32)

    def over_planes(chunk):
        total = chip_own[chunk]
        for step in range(1, chips):
            chip_copies[chunk, step].wait_recv()
            total = total + from_chips[chunk, step - 1].astype(jnp.float32)
        for part in range(4):
            piece = total[
                (part // 2) * (shard // 2) : (part // 2 + 1) * (shard // 2),
                (part % 2) * 128 : (part % 2 + 1) * 128,
            ]
            plane_wide[chunk, part] = piece
            plane_half[chunk, part] = piece.astype(jnp.bfloat16)
        for step in range(1, dp_count):
            target = lax.rem(plane + step, dp_count)
            plane_copies[chunk, step] = launch(
                send(
                    plane_half.at[chunk, target],
                    from_planes.at[chunk, step - 1],
                    plane_send.at[chunk, step - 1],
                    plane_recv.at[chunk, step - 1],
                    "dp",
                    target,
                )
            )

    def spread(chunk):
        total = plane_wide[chunk, plane]
        for step in range(1, dp_count):
            plane_copies[chunk, step].wait_recv()
            total = total + from_planes[chunk, step - 1].astype(jnp.float32)
        final[chunk, plane] = total.astype(jnp.bfloat16)
        for step in range(1, dp_count):
            target = lax.rem(plane + step, dp_count)
            final_copies[chunk, step] = launch(
                send(
                    final.at[chunk, plane],
                    final.at[chunk, plane],
                    final_send.at[chunk, step - 1],
                    final_recv.at[chunk, step - 1],
                    "dp",
                    target,
                )
            )

    def finish(chunk):
        for step in range(1, dp_count):
            final_copies[chunk, step].wait_recv()
        for part in range(4):
            weight_out[
                pl.ds((part // 2) * (shard // 2), shard // 2),
                pl.ds(chunk * width + (part % 2) * 128, 128),
            ] = final[chunk, part].astype(jnp.float32) * grad_scale

    last = chunks - 1
    forward(0)
    for copy in halos:
        copy.wait_recv()
    for chunk in range(chunks):
        project(chunk)
        if chunk >= 1:
            over_chips(chunk - 1)
        if chunk >= 2:
            over_planes(chunk - 2)
        slopes(chunk)
        if chunk < last:
            forward(chunk + 1)
        else:
            tap_pair = launch(
                send(tap_own, tap_core, tap_send.at[0], tap_recv.at[0], "seq", sibling)
            )
        back(chunk)
        weight_terms(chunk)

    for chunk in range(last - 1):
        spread(chunk)
    over_chips(last)
    over_planes(last - 1)
    tap_pair.wait_recv()
    tap_chips[chip] = tap_own[...] + tap_core[...]
    tap_row = []
    for step in range(1, chips):
        tap_row.append(
            launch(
                send(
                    tap_chips.at[chip],
                    tap_chips.at[chip],
                    tap_send.at[step],
                    tap_recv.at[step],
                    "seq",
                    2 * lax.rem(chip + step, chips) + core,
                )
            )
        )
    values = jnp.zeros((rows, channels), jnp.float32)
    for chunk in range(chunks):
        values = values + lax.dot_general(
            grad_merged[:, cols(chunk)],
            weights[chunk].reshape(channels, width),
            (((1,), (1,)), ((), ())),
            preferred_element_type=jnp.float32,
        )
    skip_out[0] = values.astype(jnp.bfloat16)
    write(skip_out, skip_hbm_out, 0)
    coarse_out[0] = jnp.dot(
        pair_mat[...], grad_merged[...], preferred_element_type=jnp.float32
    ).astype(jnp.bfloat16)
    write(coarse_out, coarse_hbm_out, 1)
    for copy in tap_row:
        copy.wait_recv()
    total = tap_chips[0]
    for block in range(1, chips):
        total = total + tap_chips[block]
    tap_planes[plane] = total
    tap_line = []
    for step in range(1, dp_count):
        tap_line.append(
            launch(
                send(
                    tap_planes.at[plane],
                    tap_planes.at[plane],
                    tap_send.at[chips - 1 + step],
                    tap_recv.at[chips - 1 + step],
                    "dp",
                    lax.rem(plane + step, dp_count),
                )
            )
        )
    over_planes(last)
    spread(last - 1)
    for copy in tap_line:
        copy.wait_recv()
    total = tap_planes[0]
    for block in range(1, dp_count):
        total = total + tap_planes[block]
    taps_out[...] = total[:3] * grad_scale
    write(taps_out, taps_hbm_out, 2)
    for chunk in range(last - 1):
        finish(chunk)
    spread(last)
    finish(last - 1)
    finish(last)
    write(weight_out, weight_hbm_out, 3)
    for copy in stores:
        copy.wait()
    for copy in sends:
        copy.wait_send()


def store(*refs):
    loads = [pltpu.make_async_copy(refs[k], refs[8 + k], refs[12].at[k]) for k in range(4)]
    writes = [pltpu.make_async_copy(refs[8 + k], refs[4 + k], refs[13].at[k]) for k in range(4)]
    for copy in loads:
        copy.start()
    for load, write in zip(loads, writes):
        load.wait()
        write.start()
    for copy in writes:
        copy.wait()


def fused(seq_count, dp_count, coarse, skip, skip_weight, depth_taps, cotangent):
    _, rows, channels = skip.shape
    shard = skip_weight.shape[0]
    chunks = channels // width
    chips = seq_count // 2
    half, wide = jnp.bfloat16, jnp.float32
    dma = pltpu.SemaphoreType.DMA
    extended = rows + 2 * halo
    results = pl.pallas_call(
        functools.partial(
            kernel, seq_count, dp_count, 1.0 / math.sqrt(rows * seq_count * dp_count)
        ),
        out_shape=(
            jax.ShapeDtypeStruct(coarse.shape, half),
            jax.ShapeDtypeStruct(skip.shape, half),
            jax.ShapeDtypeStruct(skip_weight.shape, wide),
            jax.ShapeDtypeStruct(depth_taps.shape, wide),
        ),
        in_specs=[pl.BlockSpec(memory_space=pltpu.HBM)] * 5,
        out_specs=(pl.BlockSpec(memory_space=pltpu.HBM),) * 4,
        scratch_shapes=[
            pltpu.VMEM(coarse.shape, half),
            pltpu.VMEM(skip.shape, half),
            pltpu.VMEM(skip_weight.shape, wide),
            pltpu.VMEM(depth_taps.shape, wide),
            pltpu.VMEM((extended, channels), half),
            pltpu.VMEM((extended, channels), half),
            pltpu.VMEM((rows // 2 + 2 * halo, channels), half),
            pltpu.VMEM((channels, rows), half),
            pltpu.VMEM((extended, rows // 2 + 2 * halo), half),
            pltpu.VMEM((rows // 2, rows), half),
            pltpu.VMEM((chunks, seq_count, shard, width), half),
            pltpu.VMEM((extended, width), wide),
            pltpu.VMEM((extended, width), wide),
            pltpu.VMEM((rows, channels), half),
            pltpu.VMEM((chunks, 2, chips, shard, width), wide),
            pltpu.VMEM((chunks, 2, chips, shard, width), half),
            pltpu.VMEM((chunks, chips, shard, width), half),
            pltpu.VMEM((chunks, chips, shard, width), half),
            pltpu.VMEM((chunks, shard, width), wide),
            pltpu.VMEM((chunks, chips - 1, shard, width), half),
            pltpu.VMEM((chunks, 4, shard // 2, 128), wide),
            pltpu.VMEM((chunks, 4, shard // 2, 128), half),
            pltpu.VMEM((chunks, dp_count - 1, shard // 2, 128), half),
            pltpu.VMEM((chunks, 4, shard // 2, 128), half),
            pltpu.VMEM(depth_taps.shape, wide),
            pltpu.VMEM((8, channels), wide),
            pltpu.VMEM((8, channels), wide),
            pltpu.VMEM((chips, 8, channels), wide),
            pltpu.VMEM((dp_count, 8, channels), wide),
            dma((8 + chunks,)),
            dma((6,)),
            dma((6,)),
            dma((chunks, chips - 1)),
            dma((chunks, chips - 1)),
            dma((chunks, chips - 1)),
            dma((chunks, chips - 1)),
            dma((chunks,)),
            dma((chunks,)),
            dma((chunks,)),
            dma((chunks,)),
            dma((chunks, chips - 1)),
            dma((chunks, chips - 1)),
            dma((chunks, dp_count - 1)),
            dma((chunks, dp_count - 1)),
            dma((chunks, dp_count - 1)),
            dma((chunks, dp_count - 1)),
            dma((chips + dp_count - 1,)),
            dma((chips + dp_count - 1,)),
        ],
        compiler_params=pltpu.CompilerParams(
            collective_id=0, has_side_effects=True, vmem_limit_bytes=62 * 1024 * 1024
        ),
    )(coarse, skip, skip_weight, depth_taps, cotangent)
    return pl.pallas_call(
        store,
        out_shape=tuple(jax.ShapeDtypeStruct(part.shape, part.dtype) for part in results),
        in_specs=[pl.BlockSpec(memory_space=pltpu.HBM)] * 4,
        out_specs=(pl.BlockSpec(memory_space=pltpu.HBM),) * 4,
        scratch_shapes=[pltpu.VMEM(part.shape, part.dtype) for part in results]
        + [dma((4,)), dma((4,))],
        compiler_params=pltpu.CompilerParams(vmem_limit_bytes=62 * 1024 * 1024),
    )(*results)


def solution(mesh):
    placed = (P("dp", "seq", None), P("dp", "seq", None), P("seq", None), P(), P("dp", "seq", None))
    seq_count, dp_count = mesh.shape["seq"], mesh.shape["dp"]

    def device_part(coarse, skip, skip_weight, depth_taps, cotangent):
        fits = (
            skip.shape[0] == 1
            and skip.shape[1] % tile == 0
            and skip.shape[2] % width == 0
            and skip_weight.shape[0] % 32 == 0
            and seq_count % 2 == 0
            and seq_count > 2
            and dp_count == 4
        )
        if fits:
            return fused(seq_count, dp_count, coarse, skip, skip_weight, depth_taps, cotangent)
        return local(coarse, skip, skip_weight, depth_taps, cotangent)

    return jax.shard_map(
        device_part,
        mesh=mesh,
        in_specs=placed,
        out_specs=(P("dp", "seq", None), P("dp", "seq", None), P("seq", None), P()),
        check_vma=False,
    )
```

```python
import functools
import math

import jax
import jax.numpy as jnp
from jax import lax
from jax.experimental import pallas as pl
from jax.experimental.pallas import tpu as pltpu
from jax.sharding import PartitionSpec as P

inv_root_two = 0.7071067811865476
inv_root_tau = 0.3989422804014327


def padded_2(cells, sides, width):
    for axis, dim in sides:
        count = lax.axis_size(axis)
        ends = count - 1
        head = lax.slice_in_dim(cells, 0, width, axis=dim)
        tail = lax.slice_in_dim(cells, cells.shape[dim] - width, cells.shape[dim], axis=dim)
        cells = jnp.concatenate(
            [
                lax.ppermute(tail, axis, [(i, (i + 1) % count) for i in range(ends)]),
                cells,
                lax.ppermute(head, axis, [((i + 1) % count, i) for i in range(ends)]),
            ],
            axis=dim,
        )
    return cells


def gelu_slope(pre_act):
    normal_cdf = 0.5 * (1.0 + lax.erf(pre_act * inv_root_two))
    normal_pdf = jnp.exp(-0.5 * pre_act * pre_act) * inv_root_tau
    return normal_cdf + pre_act * normal_pdf


def local(coarse, skip, skip_weight, depth_taps, cotangent):
    batch_rows, fine_rows, channels = skip.shape
    flat_count = batch_rows * fine_rows
    shard_rows = skip_weight.shape[0]
    flat_skip = skip.reshape(flat_count, channels)
    full_weight = lax.all_gather(skip_weight, "seq", axis=0, tiled=True)
    projected = jnp.dot(flat_skip, full_weight, preferred_element_type=jnp.float32)
    upsampled = jnp.broadcast_to(
        coarse[:, :, None, :], (batch_rows, fine_rows // 2, 2, channels)
    ).reshape(flat_count, channels)
    merged = (
        (upsampled.astype(jnp.float32) + projected)
        .astype(jnp.bfloat16)
        .reshape(batch_rows, fine_rows, channels)
    )
    padded = padded_2(merged, (("seq", 1),), 1)
    pre_act = (
        depth_taps[0] * padded[:, :-2]
        + depth_taps[1] * padded[:, 1:-1]
        + depth_taps[2] * padded[:, 2:]
    )
    grad_pre = (cotangent * gelu_slope(pre_act)).astype(jnp.bfloat16)
    grad_padded = padded_2(grad_pre, (("seq", 1),), 1)
    grad_merged = (
        cotangent.astype(jnp.float32)
        + depth_taps[0] * grad_padded[:, 2:]
        + depth_taps[1] * grad_padded[:, 1:-1]
        + depth_taps[2] * grad_padded[:, :-2]
    ).astype(jnp.bfloat16)
    flat_grad = grad_merged.reshape(flat_count, channels)
    grad_wide = grad_pre.astype(jnp.float32)
    tap_terms = jnp.stack(
        [
            jnp.sum(
                padded[:, offset : offset + fine_rows].astype(jnp.float32) * grad_wide, axis=(0, 1)
            )
            for offset in range(3)
        ]
    )
    grad_scale = 1.0 / math.sqrt(flat_count * lax.axis_size("seq") * lax.axis_size("dp"))
    summed, tap_sum = lax.psum(
        (
            lax.dot_general(
                flat_skip, flat_grad, (((0,), (0,)), ((), ())), preferred_element_type=jnp.float32
            ),
            tap_terms,
        ),
        ("seq", "dp"),
    )
    weight_sum = lax.dynamic_slice_in_dim(summed, lax.axis_index("seq") * shard_rows, shard_rows, 0)
    grad_skip = lax.dot_general(
        flat_grad, full_weight, (((1,), (1,)), ((), ())), preferred_element_type=jnp.float32
    )
    grad_coarse = (
        grad_merged.astype(jnp.float32)
        .reshape(batch_rows, fine_rows // 2, 2, channels)
        .sum(axis=2)
        .astype(jnp.bfloat16)
    )
    grad_skip = grad_skip.astype(jnp.bfloat16).reshape(batch_rows, fine_rows, channels)
    return (grad_coarse, grad_skip, weight_sum * grad_scale, tap_sum * grad_scale)


MESH = pl.DeviceIdType.MESH
halo = 16
tile = 64
width = 256


def send(src, dst, send_sem, recv_sem, axis, target):
    return pltpu.make_async_remote_copy(
        src_ref=src,
        dst_ref=dst,
        send_sem=send_sem,
        recv_sem=recv_sem,
        device_id={axis: target},
        device_id_type=MESH,
    )


def kernel(
    seq_count,
    dp_count,
    grad_scale,
    coarse_hbm,
    skip_hbm,
    weight_hbm,
    taps_hbm,
    cot_hbm,
    coarse_hbm_out,
    skip_hbm_out,
    weight_hbm_out,
    taps_hbm_out,
    coarse_out,
    skip_out,
    weight_out,
    taps_out,
    skip_ext,
    cot_ext,
    coarse_ext,
    skip_turned,
    repeat_mat,
    pair_mat,
    weights,
    merged,
    grad_pre,
    grad_merged,
    term_wide,
    term_half,
    from_core,
    chip_half,
    chip_own,
    from_chips,
    plane_wide,
    plane_half,
    from_planes,
    final,
    taps_ref,
    tap_own,
    tap_core,
    tap_chips,
    tap_planes,
    local_sem,
    halo_send,
    halo_recv,
    gather_send,
    gather_recv,
    forward_send,
    forward_recv,
    sib_send,
    sib_recv,
    core_send,
    core_recv,
    chip_send,
    chip_recv,
    plane_send,
    plane_recv,
    final_send,
    final_recv,
    tap_send,
    tap_recv,
):
    rows = skip_hbm.shape[1]
    channels = skip_hbm.shape[2]
    shard = weight_hbm.shape[0]
    chunks = channels // width
    chips = seq_count // 2
    me = lax.axis_index("seq")
    plane = lax.axis_index("dp")
    core = lax.rem(me, 2)
    chip = lax.div(me, 2)
    sibling = me + 1 - 2 * core
    right = lax.rem(me + 1, seq_count)
    left = lax.rem(me + seq_count - 1, seq_count)

    loads = [
        pltpu.make_async_copy(skip_hbm.at[0], skip_ext.at[pl.ds(halo, rows)], local_sem.at[0]),
        pltpu.make_async_copy(cot_hbm.at[0], cot_ext.at[pl.ds(halo, rows)], local_sem.at[1]),
        pltpu.make_async_copy(
            coarse_hbm.at[0], coarse_ext.at[pl.ds(halo, rows // 2)], local_sem.at[2]
        ),
    ]
    loads.append(pltpu.make_async_copy(taps_hbm, taps_ref, local_sem.at[3]))
    for chunk in range(channels // width):
        loads.append(
            pltpu.make_async_copy(
                weight_hbm.at[:, pl.ds(chunk * width, width)],
                weights.at[chunk, me],
                local_sem.at[4 + chunk],
            )
        )
    for copy in loads:
        copy.start()

    barrier = pltpu.get_barrier_semaphore()
    for step in range(1, seq_count):
        pl.semaphore_signal(
            barrier, inc=1, device_id={"seq": lax.rem(me + step, seq_count)}, device_id_type=MESH
        )
    for step in range(1, dp_count):
        pl.semaphore_signal(
            barrier, inc=1, device_id={"dp": lax.rem(plane + step, dp_count)}, device_id_type=MESH
        )
    pl.semaphore_wait(barrier, seq_count + dp_count - 2)

    sends = []
    stores = []

    def write(source, target, number):
        stores.append(
            pltpu.make_async_copy(source, target, local_sem.at[4 + channels // width + number])
        )
        stores[-1].start()


    def launch(copy):
        copy.start()
        sends.append(copy)
        return copy

    def cols(chunk):
        return pl.ds(chunk * width, width)

    gathers, own_halves = {}, {}

    def gather(chunk):
        for step in range(1, chips):
            target = 2 * lax.rem(chip + step, chips) + core
            gathers[chunk, step] = launch(
                send(
                    weight_hbm.at[:, cols(chunk)],
                    weights.at[chunk, me],
                    gather_send.at[chunk, step - 1],
                    gather_recv.at[chunk, step - 1],
                    "seq",
                    target,
                )
            )
        own_halves[chunk] = launch(
            send(
                weight_hbm.at[:, cols(chunk)],
                weights.at[chunk, me],
                sib_send.at[chunk],
                sib_recv.at[chunk],
                "seq",
                sibling,
            )
        )

    gather(0)
    halos = []
    pairs = ((skip_hbm, skip_ext, rows), (coarse_hbm, coarse_ext, rows // 2), (cot_hbm, cot_ext, rows))
    for number, (source, target, count) in enumerate(pairs):
        halos.append(
            launch(
                send(
                    source.at[0, pl.ds(count - halo, halo)],
                    target.at[pl.ds(0, halo)],
                    halo_send.at[2 * number],
                    halo_recv.at[2 * number],
                    "seq",
                    right,
                )
            )
        )
        halos.append(
            launch(
                send(
                    source.at[0, pl.ds(0, halo)],
                    target.at[pl.ds(count + halo, halo)],
                    halo_send.at[2 * number + 1],
                    halo_recv.at[2 * number + 1],
                    "seq",
                    left,
                )
            )
        )
    for chunk in range(1, chunks):
        gather(chunk)

    out_row = lax.broadcasted_iota(jnp.int32, repeat_mat.shape, 0)
    in_row = lax.broadcasted_iota(jnp.int32, repeat_mat.shape, 1)
    repeat_mat[...] = jnp.where(
        lax.shift_right_logical(out_row, 1) + halo // 2 == in_row, 1.0, 0.0
    ).astype(jnp.bfloat16)
    out_row = lax.broadcasted_iota(jnp.int32, pair_mat.shape, 0)
    in_row = lax.broadcasted_iota(jnp.int32, pair_mat.shape, 1)
    pair_mat[...] = jnp.where(lax.shift_right_logical(in_row, 1) == out_row, 1.0, 0.0).astype(
        jnp.bfloat16
    )
    tap_own[...] = jnp.zeros_like(tap_own)
    for copy in loads:
        copy.wait()
    skip_turned[...] = skip_ext[pl.ds(halo, rows), :].T

    low_in = jnp.where(me == 0, 0.0, 1.0)
    high_in = jnp.where(me == seq_count - 1, 0.0, 1.0)
    forwards = {}

    def forward(chunk):
        for step in range(1, chips):
            gathers[chunk, step].wait_recv()
            owner = 2 * lax.rem(chip + chips - step, chips) + core
            forwards[chunk, step] = launch(
                send(
                    weights.at[chunk, owner],
                    weights.at[chunk, owner],
                    forward_send.at[chunk, step - 1],
                    forward_recv.at[chunk, step - 1],
                    "seq",
                    sibling,
                )
            )

    def project(chunk):
        own_halves[chunk].wait_recv()
        for step in range(1, chips):
            forwards[chunk, step].wait_recv()
        dense = weights[chunk].reshape(channels, width)
        values = jnp.dot(skip_ext[...], dense, preferred_element_type=jnp.float32) + jnp.dot(
            repeat_mat[...], coarse_ext[:, cols(chunk)], preferred_element_type=jnp.float32
        )
        values = values.astype(jnp.bfloat16).astype(jnp.float32)
        merged[pl.ds(0, halo), :] = values[:halo] * low_in
        merged[pl.ds(halo, rows), :] = values[halo : halo + rows]
        merged[pl.ds(halo + rows, halo), :] = values[halo + rows :] * high_in

    def slopes(chunk):
        tap = [taps_ref[pl.ds(k, 1), cols(chunk)] for k in range(3)]

        def one(first, count, cot):
            near = [merged[pl.ds(first + k - 1, count), :] for k in range(3)]
            pre_act = tap[0] * near[0] + tap[1] * near[1] + tap[2] * near[2]
            return near, (cot * gelu_slope(pre_act)).astype(jnp.bfloat16).astype(jnp.float32)

        edge = cot_ext[pl.ds(0, halo), cols(chunk)].astype(jnp.float32)
        grad_pre[pl.ds(8, 8), :] = one(8, 8, edge[8:])[1] * low_in
        edge = cot_ext[pl.ds(halo + rows, halo), cols(chunk)].astype(jnp.float32)
        grad_pre[pl.ds(halo + rows, 8), :] = one(halo + rows, 8, edge[:8])[1] * high_in

        def body(number, totals):
            first = halo + number * tile
            cot = cot_ext[pl.ds(first, tile), cols(chunk)].astype(jnp.float32)
            near, grad = one(first, tile, cot)
            grad_pre[pl.ds(first, tile), :] = grad
            return tuple(
                total + jnp.sum((part * grad).reshape(tile // 8, 8, width), axis=0)
                for total, part in zip(totals, near)
            )

        zero = jnp.zeros((8, width), jnp.float32)
        totals = (zero, zero, zero)
        for number in range(rows // tile):
            totals = body(number, totals)
        for k in range(3):
            tap_own[pl.ds(k, 1), cols(chunk)] = jnp.sum(totals[k], axis=0, keepdims=True)

    def back(chunk):
        tap = [taps_ref[pl.ds(k, 1), cols(chunk)] for k in range(3)]

        for number in range(rows // tile):
            first = halo + number * tile
            cot = cot_ext[pl.ds(first, tile), cols(chunk)].astype(jnp.float32)
            grad_merged[pl.ds(first - halo, tile), cols(chunk)] = (
                cot
                + tap[0] * grad_pre[pl.ds(first + 1, tile), :]
                + tap[1] * grad_pre[pl.ds(first, tile), :]
                + tap[2] * grad_pre[pl.ds(first - 1, tile), :]
            ).astype(jnp.bfloat16)

    core_copies, chip_copies, plane_copies, final_copies = {}, {}, {}, {}

    def weight_terms(chunk):
        terms = jnp.dot(
            skip_turned[...], grad_merged[:, cols(chunk)], preferred_element_type=jnp.float32
        )
        for block in range(seq_count):
            part = terms[block * shard : (block + 1) * shard]
            term_wide[chunk, block % 2, block // 2] = part
            term_half[chunk, block % 2, block // 2] = part.astype(jnp.bfloat16)
        core_copies[chunk] = launch(
            send(
                term_half.at[chunk, 1 - core],
                from_core.at[chunk],
                core_send.at[chunk],
                core_recv.at[chunk],
                "seq",
                sibling,
            )
        )

    def over_chips(chunk):
        core_copies[chunk].wait_recv()
        for block in range(chips):
            chip_half[chunk, block] = (
                term_wide[chunk, core, block] + from_core[chunk, block].astype(jnp.float32)
            ).astype(jnp.bfloat16)
        for step in range(1, chips):
            target = lax.rem(chip + step, chips)
            chip_copies[chunk, step] = launch(
                send(
                    chip_half.at[chunk, target],
                    from_chips.at[chunk, step - 1],
                    chip_send.at[chunk, step - 1],
                    chip_recv.at[chunk, step - 1],
                    "seq",
                    2 * target + core,
                )
            )
        chip_own[chunk] = term_wide[chunk, core, chip] + from_core[chunk, chip].astype(jnp.float32)

    def over_planes(chunk):
        total = chip_own[chunk]
        for step in range(1, chips):
            chip_copies[chunk, step].wait_recv()
            total = total + from_chips[chunk, step - 1].astype(jnp.float32)
        for part in range(4):
            piece = total[
                (part // 2) * (shard // 2) : (part // 2 + 1) * (shard // 2),
                (part % 2) * 128 : (part % 2 + 1) * 128,
            ]
            plane_wide[chunk, part] = piece
            plane_half[chunk, part] = piece.astype(jnp.bfloat16)
        for step in range(1, dp_count):
            target = lax.rem(plane + step, dp_count)
            plane_copies[chunk, step] = launch(
                send(
                    plane_half.at[chunk, target],
                    from_planes.at[chunk, step - 1],
                    plane_send.at[chunk, step - 1],
                    plane_recv.at[chunk, step - 1],
                    "dp",
                    target,
                )
            )

    def spread(chunk):
        total = plane_wide[chunk, plane]
        for step in range(1, dp_count):
            plane_copies[chunk, step].wait_recv()
            total = total + from_planes[chunk, step - 1].astype(jnp.float32)
        final[chunk, plane] = total.astype(jnp.bfloat16)
        for step in range(1, dp_count):
            target = lax.rem(plane + step, dp_count)
            final_copies[chunk, step] = launch(
                send(
                    final.at[chunk, plane],
                    final.at[chunk, plane],
                    final_send.at[chunk, step - 1],
                    final_recv.at[chunk, step - 1],
                    "dp",
                    target,
                )
            )

    def finish(chunk):
        for step in range(1, dp_count):
            final_copies[chunk, step].wait_recv()
        for part in range(4):
            weight_out[
                pl.ds((part // 2) * (shard // 2), shard // 2),
                pl.ds(chunk * width + (part % 2) * 128, 128),
            ] = final[chunk, part].astype(jnp.float32) * grad_scale

    last = chunks - 1
    forward(0)
    for copy in halos:
        copy.wait_recv()
    for chunk in range(chunks):
        project(chunk)
        if chunk >= 1:
            over_chips(chunk - 1)
        if chunk >= 2:
            over_planes(chunk - 2)
        slopes(chunk)
        if chunk < last:
            forward(chunk + 1)
        else:
            tap_pair = launch(
                send(tap_own, tap_core, tap_send.at[0], tap_recv.at[0], "seq", sibling)
            )
        back(chunk)
        weight_terms(chunk)

    over_chips(last)
    over_planes(last - 1)
    tap_pair.wait_recv()
    tap_chips[chip] = tap_own[...] + tap_core[...]
    tap_row = []
    for step in range(1, chips):
        tap_row.append(
            launch(
                send(
                    tap_chips.at[chip],
                    tap_chips.at[chip],
                    tap_send.at[step],
                    tap_recv.at[step],
                    "seq",
                    2 * lax.rem(chip + step, chips) + core,
                )
            )
        )
    for chunk in range(last - 1):
        spread(chunk)
    values = jnp.zeros((rows, channels), jnp.float32)
    for chunk in range(chunks):
        values = values + lax.dot_general(
            grad_merged[:, cols(chunk)],
            weights[chunk].reshape(channels, width),
            (((1,), (1,)), ((), ())),
            preferred_element_type=jnp.float32,
        )
    skip_out[0] = values.astype(jnp.bfloat16)
    write(skip_out, skip_hbm_out, 0)
    coarse_out[0] = jnp.dot(
        pair_mat[...], grad_merged[...], preferred_element_type=jnp.float32
    ).astype(jnp.bfloat16)
    write(coarse_out, coarse_hbm_out, 1)
    over_planes(last)
    for copy in tap_row:
        copy.wait_recv()
    total = tap_chips[0]
    for block in range(1, chips):
        total = total + tap_chips[block]
    tap_planes[plane] = total
    tap_line = []
    for step in range(1, dp_count):
        tap_line.append(
            launch(
                send(
                    tap_planes.at[plane],
                    tap_planes.at[plane],
                    tap_send.at[chips - 1 + step],
                    tap_recv.at[chips - 1 + step],
                    "dp",
                    lax.rem(plane + step, dp_count),
                )
            )
        )
    spread(last - 1)
    for chunk in range(last - 1):
        finish(chunk)
    spread(last)
    finish(last - 1)
    for copy in tap_line:
        copy.wait_recv()
    total = tap_planes[0]
    for block in range(1, dp_count):
        total = total + tap_planes[block]
    taps_out[...] = total[:3] * grad_scale
    write(taps_out, taps_hbm_out, 2)
    finish(last)
    write(weight_out, weight_hbm_out, 3)
    for copy in stores:
        copy.wait()
    for copy in sends:
        copy.wait_send()


def store(*refs):
    loads = [pltpu.make_async_copy(refs[k], refs[8 + k], refs[12].at[k]) for k in range(4)]
    writes = [pltpu.make_async_copy(refs[8 + k], refs[4 + k], refs[13].at[k]) for k in range(4)]
    for copy in loads:
        copy.start()
    for load, write in zip(loads, writes):
        load.wait()
        write.start()
    for copy in writes:
        copy.wait()


def fused(seq_count, dp_count, coarse, skip, skip_weight, depth_taps, cotangent):
    _, rows, channels = skip.shape
    shard = skip_weight.shape[0]
    chunks = channels // width
    chips = seq_count // 2
    half, wide = jnp.bfloat16, jnp.float32
    dma = pltpu.SemaphoreType.DMA
    extended = rows + 2 * halo
    results = pl.pallas_call(
        functools.partial(
            kernel, seq_count, dp_count, 1.0 / math.sqrt(rows * seq_count * dp_count)
        ),
        out_shape=(
            jax.ShapeDtypeStruct(coarse.shape, half),
            jax.ShapeDtypeStruct(skip.shape, half),
            jax.ShapeDtypeStruct(skip_weight.shape, wide),
            jax.ShapeDtypeStruct(depth_taps.shape, wide),
        ),
        in_specs=[pl.BlockSpec(memory_space=pltpu.HBM)] * 5,
        out_specs=(pl.BlockSpec(memory_space=pltpu.HBM),) * 4,
        scratch_shapes=[
            pltpu.VMEM(coarse.shape, half),
            pltpu.VMEM(skip.shape, half),
            pltpu.VMEM(skip_weight.shape, wide),
            pltpu.VMEM(depth_taps.shape, wide),
            pltpu.VMEM((extended, channels), half),
            pltpu.VMEM((extended, channels), half),
            pltpu.VMEM((rows // 2 + 2 * halo, channels), half),
            pltpu.VMEM((channels, rows), half),
            pltpu.VMEM((extended, rows // 2 + 2 * halo), half),
            pltpu.VMEM((rows // 2, rows), half),
            pltpu.VMEM((chunks, seq_count, shard, width), half),
            pltpu.VMEM((extended, width), wide),
            pltpu.VMEM((extended, width), wide),
            pltpu.VMEM((rows, channels), half),
            pltpu.VMEM((chunks, 2, chips, shard, width), wide),
            pltpu.VMEM((chunks, 2, chips, shard, width), half),
            pltpu.VMEM((chunks, chips, shard, width), half),
            pltpu.VMEM((chunks, chips, shard, width), half),
            pltpu.VMEM((chunks, shard, width), wide),
            pltpu.VMEM((chunks, chips - 1, shard, width), half),
            pltpu.VMEM((chunks, 4, shard // 2, 128), wide),
            pltpu.VMEM((chunks, 4, shard // 2, 128), half),
            pltpu.VMEM((chunks, dp_count - 1, shard // 2, 128), half),
            pltpu.VMEM((chunks, 4, shard // 2, 128), half),
            pltpu.VMEM(depth_taps.shape, wide),
            pltpu.VMEM((8, channels), wide),
            pltpu.VMEM((8, channels), wide),
            pltpu.VMEM((chips, 8, channels), wide),
            pltpu.VMEM((dp_count, 8, channels), wide),
            dma((8 + chunks,)),
            dma((6,)),
            dma((6,)),
            dma((chunks, chips - 1)),
            dma((chunks, chips - 1)),
            dma((chunks, chips - 1)),
            dma((chunks, chips - 1)),
            dma((chunks,)),
            dma((chunks,)),
            dma((chunks,)),
            dma((chunks,)),
            dma((chunks, chips - 1)),
            dma((chunks, chips - 1)),
            dma((chunks, dp_count - 1)),
            dma((chunks, dp_count - 1)),
            dma((chunks, dp_count - 1)),
            dma((chunks, dp_count - 1)),
            dma((chips + dp_count - 1,)),
            dma((chips + dp_count - 1,)),
        ],
        compiler_params=pltpu.CompilerParams(
            collective_id=0, has_side_effects=True, vmem_limit_bytes=62 * 1024 * 1024
        ),
    )(coarse, skip, skip_weight, depth_taps, cotangent)
    return pl.pallas_call(
        store,
        out_shape=tuple(jax.ShapeDtypeStruct(part.shape, part.dtype) for part in results),
        in_specs=[pl.BlockSpec(memory_space=pltpu.HBM)] * 4,
        out_specs=(pl.BlockSpec(memory_space=pltpu.HBM),) * 4,
        scratch_shapes=[pltpu.VMEM(part.shape, part.dtype) for part in results]
        + [dma((4,)), dma((4,))],
        compiler_params=pltpu.CompilerParams(vmem_limit_bytes=62 * 1024 * 1024),
    )(*results)


def solution(mesh):
    placed = (P("dp", "seq", None), P("dp", "seq", None), P("seq", None), P(), P("dp", "seq", None))
    seq_count, dp_count = mesh.shape["seq"], mesh.shape["dp"]

    def device_part(coarse, skip, skip_weight, depth_taps, cotangent):
        fits = (
            skip.shape[0] == 1
            and skip.shape[1] % tile == 0
            and skip.shape[2] % width == 0
            and skip_weight.shape[0] % 32 == 0
            and seq_count % 2 == 0
            and seq_count > 2
            and dp_count == 4
        )
        if fits:
            return fused(seq_count, dp_count, coarse, skip, skip_weight, depth_taps, cotangent)
        return local(coarse, skip, skip_weight, depth_taps, cotangent)

    return jax.shard_map(
        device_part,
        mesh=mesh,
        in_specs=placed,
        out_specs=(P("dp", "seq", None), P("dp", "seq", None), P("seq", None), P()),
        check_vma=False,
    )
```

```python
import functools
import math

import jax
import jax.numpy as jnp
from jax import lax
from jax.experimental import pallas as pl
from jax.experimental.pallas import tpu as pltpu
from jax.sharding import PartitionSpec as P

inv_root_two = 0.7071067811865476
inv_root_tau = 0.3989422804014327


def padded_2(cells, sides, width):
    for axis, dim in sides:
        count = lax.axis_size(axis)
        ends = count - 1
        head = lax.slice_in_dim(cells, 0, width, axis=dim)
        tail = lax.slice_in_dim(cells, cells.shape[dim] - width, cells.shape[dim], axis=dim)
        cells = jnp.concatenate(
            [
                lax.ppermute(tail, axis, [(i, (i + 1) % count) for i in range(ends)]),
                cells,
                lax.ppermute(head, axis, [((i + 1) % count, i) for i in range(ends)]),
            ],
            axis=dim,
        )
    return cells


def gelu_slope(pre_act):
    normal_cdf = 0.5 * (1.0 + lax.erf(pre_act * inv_root_two))
    normal_pdf = jnp.exp(-0.5 * pre_act * pre_act) * inv_root_tau
    return normal_cdf + pre_act * normal_pdf


def local(coarse, skip, skip_weight, depth_taps, cotangent):
    batch_rows, fine_rows, channels = skip.shape
    flat_count = batch_rows * fine_rows
    shard_rows = skip_weight.shape[0]
    flat_skip = skip.reshape(flat_count, channels)
    full_weight = lax.all_gather(skip_weight, "seq", axis=0, tiled=True)
    projected = jnp.dot(flat_skip, full_weight, preferred_element_type=jnp.float32)
    upsampled = jnp.broadcast_to(
        coarse[:, :, None, :], (batch_rows, fine_rows // 2, 2, channels)
    ).reshape(flat_count, channels)
    merged = (
        (upsampled.astype(jnp.float32) + projected)
        .astype(jnp.bfloat16)
        .reshape(batch_rows, fine_rows, channels)
    )
    padded = padded_2(merged, (("seq", 1),), 1)
    pre_act = (
        depth_taps[0] * padded[:, :-2]
        + depth_taps[1] * padded[:, 1:-1]
        + depth_taps[2] * padded[:, 2:]
    )
    grad_pre = (cotangent * gelu_slope(pre_act)).astype(jnp.bfloat16)
    grad_padded = padded_2(grad_pre, (("seq", 1),), 1)
    grad_merged = (
        cotangent.astype(jnp.float32)
        + depth_taps[0] * grad_padded[:, 2:]
        + depth_taps[1] * grad_padded[:, 1:-1]
        + depth_taps[2] * grad_padded[:, :-2]
    ).astype(jnp.bfloat16)
    flat_grad = grad_merged.reshape(flat_count, channels)
    grad_wide = grad_pre.astype(jnp.float32)
    tap_terms = jnp.stack(
        [
            jnp.sum(
                padded[:, offset : offset + fine_rows].astype(jnp.float32) * grad_wide, axis=(0, 1)
            )
            for offset in range(3)
        ]
    )
    grad_scale = 1.0 / math.sqrt(flat_count * lax.axis_size("seq") * lax.axis_size("dp"))
    summed, tap_sum = lax.psum(
        (
            lax.dot_general(
                flat_skip, flat_grad, (((0,), (0,)), ((), ())), preferred_element_type=jnp.float32
            ),
            tap_terms,
        ),
        ("seq", "dp"),
    )
    weight_sum = lax.dynamic_slice_in_dim(summed, lax.axis_index("seq") * shard_rows, shard_rows, 0)
    grad_skip = lax.dot_general(
        flat_grad, full_weight, (((1,), (1,)), ((), ())), preferred_element_type=jnp.float32
    )
    grad_coarse = (
        grad_merged.astype(jnp.float32)
        .reshape(batch_rows, fine_rows // 2, 2, channels)
        .sum(axis=2)
        .astype(jnp.bfloat16)
    )
    grad_skip = grad_skip.astype(jnp.bfloat16).reshape(batch_rows, fine_rows, channels)
    return (grad_coarse, grad_skip, weight_sum * grad_scale, tap_sum * grad_scale)


MESH = pl.DeviceIdType.MESH
halo = 16
tile = 64
width = 256


def send(src, dst, send_sem, recv_sem, axis, target):
    return pltpu.make_async_remote_copy(
        src_ref=src,
        dst_ref=dst,
        send_sem=send_sem,
        recv_sem=recv_sem,
        device_id={axis: target},
        device_id_type=MESH,
    )


def kernel(
    seq_count,
    dp_count,
    grad_scale,
    coarse_hbm,
    skip_hbm,
    weight_hbm,
    taps_hbm,
    cot_hbm,
    coarse_hbm_out,
    skip_hbm_out,
    weight_hbm_out,
    taps_hbm_out,
    coarse_out,
    skip_out,
    weight_out,
    taps_out,
    skip_ext,
    cot_ext,
    coarse_ext,
    skip_turned,
    repeat_mat,
    pair_mat,
    weights,
    merged,
    grad_pre,
    grad_merged,
    term_wide,
    term_half,
    from_core,
    chip_half,
    chip_own,
    from_chips,
    plane_wide,
    plane_half,
    from_planes,
    final,
    taps_ref,
    tap_own,
    tap_core,
    tap_chips,
    tap_planes,
    local_sem,
    halo_send,
    halo_recv,
    gather_send,
    gather_recv,
    forward_send,
    forward_recv,
    sib_send,
    sib_recv,
    core_send,
    core_recv,
    chip_send,
    chip_recv,
    plane_send,
    plane_recv,
    final_send,
    final_recv,
    tap_send,
    tap_recv,
):
    rows = skip_hbm.shape[1]
    channels = skip_hbm.shape[2]
    shard = weight_hbm.shape[0]
    chunks = channels // width
    chips = seq_count // 2
    me = lax.axis_index("seq")
    plane = lax.axis_index("dp")
    core = lax.rem(me, 2)
    chip = lax.div(me, 2)
    sibling = me + 1 - 2 * core
    right = lax.rem(me + 1, seq_count)
    left = lax.rem(me + seq_count - 1, seq_count)

    loads = [
        pltpu.make_async_copy(skip_hbm.at[0], skip_ext.at[pl.ds(halo, rows)], local_sem.at[0]),
        pltpu.make_async_copy(cot_hbm.at[0], cot_ext.at[pl.ds(halo, rows)], local_sem.at[1]),
        pltpu.make_async_copy(
            coarse_hbm.at[0], coarse_ext.at[pl.ds(halo, rows // 2)], local_sem.at[2]
        ),
    ]
    loads.append(pltpu.make_async_copy(taps_hbm, taps_ref, local_sem.at[3]))
    for chunk in range(channels // width):
        loads.append(
            pltpu.make_async_copy(
                weight_hbm.at[:, pl.ds(chunk * width, width)],
                weights.at[chunk, me],
                local_sem.at[4 + chunk],
            )
        )
    for copy in loads:
        copy.start()

    barrier = pltpu.get_barrier_semaphore()
    for step in range(1, seq_count):
        pl.semaphore_signal(
            barrier, inc=1, device_id={"seq": lax.rem(me + step, seq_count)}, device_id_type=MESH
        )
    for step in range(1, dp_count):
        pl.semaphore_signal(
            barrier, inc=1, device_id={"dp": lax.rem(plane + step, dp_count)}, device_id_type=MESH
        )
    pl.semaphore_wait(barrier, seq_count + dp_count - 2)

    sends = []
    stores = []

    def write(source, target, number):
        stores.append(
            pltpu.make_async_copy(source, target, local_sem.at[4 + channels // width + number])
        )
        stores[-1].start()


    def launch(copy):
        copy.start()
        sends.append(copy)
        return copy

    def cols(chunk):
        return pl.ds(chunk * width, width)

    gathers, own_halves = {}, {}

    def gather(chunk):
        for step in range(1, chips):
            target = 2 * lax.rem(chip + step, chips) + core
            gathers[chunk, step] = launch(
                send(
                    weight_hbm.at[:, cols(chunk)],
                    weights.at[chunk, me],
                    gather_send.at[chunk, step - 1],
                    gather_recv.at[chunk, step - 1],
                    "seq",
                    target,
                )
            )
        own_halves[chunk] = launch(
            send(
                weight_hbm.at[:, cols(chunk)],
                weights.at[chunk, me],
                sib_send.at[chunk],
                sib_recv.at[chunk],
                "seq",
                sibling,
            )
        )

    gather(0)
    halos = []
    pairs = ((skip_hbm, skip_ext, rows), (coarse_hbm, coarse_ext, rows // 2), (cot_hbm, cot_ext, rows))
    for number, (source, target, count) in enumerate(pairs):
        halos.append(
            launch(
                send(
                    source.at[0, pl.ds(count - halo, halo)],
                    target.at[pl.ds(0, halo)],
                    halo_send.at[2 * number],
                    halo_recv.at[2 * number],
                    "seq",
                    right,
                )
            )
        )
        halos.append(
            launch(
                send(
                    source.at[0, pl.ds(0, halo)],
                    target.at[pl.ds(count + halo, halo)],
                    halo_send.at[2 * number + 1],
                    halo_recv.at[2 * number + 1],
                    "seq",
                    left,
                )
            )
        )
    for chunk in range(1, chunks):
        gather(chunk)

    out_row = lax.broadcasted_iota(jnp.int32, repeat_mat.shape, 0)
    in_row = lax.broadcasted_iota(jnp.int32, repeat_mat.shape, 1)
    repeat_mat[...] = jnp.where(
        lax.shift_right_logical(out_row, 1) + halo // 2 == in_row, 1.0, 0.0
    ).astype(jnp.bfloat16)
    out_row = lax.broadcasted_iota(jnp.int32, pair_mat.shape, 0)
    in_row = lax.broadcasted_iota(jnp.int32, pair_mat.shape, 1)
    pair_mat[...] = jnp.where(lax.shift_right_logical(in_row, 1) == out_row, 1.0, 0.0).astype(
        jnp.bfloat16
    )
    tap_own[...] = jnp.zeros_like(tap_own)
    for copy in loads:
        copy.wait()
    skip_turned[...] = skip_ext[pl.ds(halo, rows), :].T

    low_in = jnp.where(me == 0, 0.0, 1.0)
    high_in = jnp.where(me == seq_count - 1, 0.0, 1.0)
    forwards = {}

    def forward(chunk):
        for step in range(1, chips):
            gathers[chunk, step].wait_recv()
            owner = 2 * lax.rem(chip + chips - step, chips) + core
            forwards[chunk, step] = launch(
                send(
                    weights.at[chunk, owner],
                    weights.at[chunk, owner],
                    forward_send.at[chunk, step - 1],
                    forward_recv.at[chunk, step - 1],
                    "seq",
                    sibling,
                )
            )

    def project(chunk):
        own_halves[chunk].wait_recv()
        for step in range(1, chips):
            forwards[chunk, step].wait_recv()
        dense = weights[chunk].reshape(channels, width)
        values = jnp.dot(skip_ext[...], dense, preferred_element_type=jnp.float32) + jnp.dot(
            repeat_mat[...], coarse_ext[:, cols(chunk)], preferred_element_type=jnp.float32
        )
        values = values.astype(jnp.bfloat16).astype(jnp.float32)
        merged[pl.ds(0, halo), :] = values[:halo] * low_in
        merged[pl.ds(halo, rows), :] = values[halo : halo + rows]
        merged[pl.ds(halo + rows, halo), :] = values[halo + rows :] * high_in

    def slopes(chunk):
        tap = [taps_ref[pl.ds(k, 1), cols(chunk)] for k in range(3)]

        def one(first, count, cot):
            near = [merged[pl.ds(first + k - 1, count), :] for k in range(3)]
            pre_act = tap[0] * near[0] + tap[1] * near[1] + tap[2] * near[2]
            return near, (cot * gelu_slope(pre_act)).astype(jnp.bfloat16).astype(jnp.float32)

        edge = cot_ext[pl.ds(0, halo), cols(chunk)].astype(jnp.float32)
        grad_pre[pl.ds(8, 8), :] = one(8, 8, edge[8:])[1] * low_in
        edge = cot_ext[pl.ds(halo + rows, halo), cols(chunk)].astype(jnp.float32)
        grad_pre[pl.ds(halo + rows, 8), :] = one(halo + rows, 8, edge[:8])[1] * high_in

        def body(number, totals):
            first = halo + number * tile
            cot = cot_ext[pl.ds(first, tile), cols(chunk)].astype(jnp.float32)
            near, grad = one(first, tile, cot)
            grad_pre[pl.ds(first, tile), :] = grad
            return tuple(
                total + jnp.sum((part * grad).reshape(tile // 8, 8, width), axis=0)
                for total, part in zip(totals, near)
            )

        zero = jnp.zeros((8, width), jnp.float32)
        totals = (zero, zero, zero)
        for number in range(rows // tile):
            totals = body(number, totals)
        for k in range(3):
            tap_own[pl.ds(k, 1), cols(chunk)] = jnp.sum(totals[k], axis=0, keepdims=True)

    def back(chunk):
        tap = [taps_ref[pl.ds(k, 1), cols(chunk)] for k in range(3)]

        for number in range(rows // tile):
            first = halo + number * tile
            cot = cot_ext[pl.ds(first, tile), cols(chunk)].astype(jnp.float32)
            grad_merged[pl.ds(first - halo, tile), cols(chunk)] = (
                cot
                + tap[0] * grad_pre[pl.ds(first + 1, tile), :]
                + tap[1] * grad_pre[pl.ds(first, tile), :]
                + tap[2] * grad_pre[pl.ds(first - 1, tile), :]
            ).astype(jnp.bfloat16)

    core_copies, chip_copies, plane_copies, final_copies = {}, {}, {}, {}

    def weight_terms(chunk):
        terms = jnp.dot(
            skip_turned[...], grad_merged[:, cols(chunk)], preferred_element_type=jnp.float32
        )
        for block in range(seq_count):
            part = terms[block * shard : (block + 1) * shard]
            term_wide[chunk, block % 2, block // 2] = part
            term_half[chunk, block % 2, block // 2] = part.astype(jnp.bfloat16)
        core_copies[chunk] = launch(
            send(
                term_half.at[chunk, 1 - core],
                from_core.at[chunk],
                core_send.at[chunk],
                core_recv.at[chunk],
                "seq",
                sibling,
            )
        )

    def over_chips(chunk):
        core_copies[chunk].wait_recv()
        for block in range(chips):
            chip_half[chunk, block] = (
                term_wide[chunk, core, block] + from_core[chunk, block].astype(jnp.float32)
            ).astype(jnp.bfloat16)
        for step in range(1, chips):
            target = lax.rem(chip + step, chips)
            chip_copies[chunk, step] = launch(
                send(
                    chip_half.at[chunk, target],
                    from_chips.at[chunk, step - 1],
                    chip_send.at[chunk, step - 1],
                    chip_recv.at[chunk, step - 1],
                    "seq",
                    2 * target + core,
                )
            )
        chip_own[chunk] = term_wide[chunk, core, chip] + from_core[chunk, chip].astype(jnp.float32)

    def over_planes(chunk):
        total = chip_own[chunk]
        for step in range(1, chips):
            chip_copies[chunk, step].wait_recv()
            total = total + from_chips[chunk, step - 1].astype(jnp.float32)
        for part in range(4):
            piece = total[
                (part // 2) * (shard // 2) : (part // 2 + 1) * (shard // 2),
                (part % 2) * 128 : (part % 2 + 1) * 128,
            ]
            plane_wide[chunk, part] = piece
            plane_half[chunk, part] = piece.astype(jnp.bfloat16)
        for step in range(1, dp_count):
            target = lax.rem(plane + step, dp_count)
            plane_copies[chunk, step] = launch(
                send(
                    plane_half.at[chunk, target],
                    from_planes.at[chunk, step - 1],
                    plane_send.at[chunk, step - 1],
                    plane_recv.at[chunk, step - 1],
                    "dp",
                    target,
                )
            )

    def spread(chunk):
        total = plane_wide[chunk, plane]
        for step in range(1, dp_count):
            plane_copies[chunk, step].wait_recv()
            total = total + from_planes[chunk, step - 1].astype(jnp.float32)
        final[chunk, plane] = total.astype(jnp.bfloat16)
        for step in range(1, dp_count):
            target = lax.rem(plane + step, dp_count)
            final_copies[chunk, step] = launch(
                send(
                    final.at[chunk, plane],
                    final.at[chunk, plane],
                    final_send.at[chunk, step - 1],
                    final_recv.at[chunk, step - 1],
                    "dp",
                    target,
                )
            )

    def finish(chunk):
        for step in range(1, dp_count):
            final_copies[chunk, step].wait_recv()
        for part in range(4):
            weight_out[
                pl.ds((part // 2) * (shard // 2), shard // 2),
                pl.ds(chunk * width + (part % 2) * 128, 128),
            ] = final[chunk, part].astype(jnp.float32) * grad_scale

    last = chunks - 1
    forward(0)
    for copy in halos:
        copy.wait_recv()
    for chunk in range(chunks):
        project(chunk)
        if chunk >= 1:
            over_chips(chunk - 1)
        slopes(chunk)
        if chunk >= 2:
            over_planes(chunk - 2)
        if chunk < last:
            forward(chunk + 1)
        else:
            tap_pair = launch(
                send(tap_own, tap_core, tap_send.at[0], tap_recv.at[0], "seq", sibling)
            )
        back(chunk)
        weight_terms(chunk)

    over_chips(last)
    over_planes(last - 1)
    tap_pair.wait_recv()
    tap_chips[chip] = tap_own[...] + tap_core[...]
    tap_row = []
    for step in range(1, chips):
        tap_row.append(
            launch(
                send(
                    tap_chips.at[chip],
                    tap_chips.at[chip],
                    tap_send.at[step],
                    tap_recv.at[step],
                    "seq",
                    2 * lax.rem(chip + step, chips) + core,
                )
            )
        )
    for chunk in range(last - 1):
        spread(chunk)
    values = jnp.zeros((rows, channels), jnp.float32)
    for chunk in range(chunks):
        values = values + lax.dot_general(
            grad_merged[:, cols(chunk)],
            weights[chunk].reshape(channels, width),
            (((1,), (1,)), ((), ())),
            preferred_element_type=jnp.float32,
        )
    skip_out[0] = values.astype(jnp.bfloat16)
    write(skip_out, skip_hbm_out, 0)
    coarse_out[0] = jnp.dot(
        pair_mat[...], grad_merged[...], preferred_element_type=jnp.float32
    ).astype(jnp.bfloat16)
    write(coarse_out, coarse_hbm_out, 1)
    over_planes(last)
    for copy in tap_row:
        copy.wait_recv()
    total = tap_chips[0]
    for block in range(1, chips):
        total = total + tap_chips[block]
    tap_planes[plane] = total
    tap_line = []
    for step in range(1, dp_count):
        tap_line.append(
            launch(
                send(
                    tap_planes.at[plane],
                    tap_planes.at[plane],
                    tap_send.at[chips - 1 + step],
                    tap_recv.at[chips - 1 + step],
                    "dp",
                    lax.rem(plane + step, dp_count),
                )
            )
        )
    spread(last - 1)
    for chunk in range(last - 1):
        finish(chunk)
    spread(last)
    finish(last - 1)
    for copy in tap_line:
        copy.wait_recv()
    total = tap_planes[0]
    for block in range(1, dp_count):
        total = total + tap_planes[block]
    taps_out[...] = total[:3] * grad_scale
    write(taps_out, taps_hbm_out, 2)
    finish(last)
    write(weight_out, weight_hbm_out, 3)
    for copy in stores:
        copy.wait()
    for copy in sends:
        copy.wait_send()


def store(*refs):
    loads = [pltpu.make_async_copy(refs[k], refs[8 + k], refs[12].at[k]) for k in range(4)]
    writes = [pltpu.make_async_copy(refs[8 + k], refs[4 + k], refs[13].at[k]) for k in range(4)]
    for copy in loads:
        copy.start()
    for load, write in zip(loads, writes):
        load.wait()
        write.start()
    for copy in writes:
        copy.wait()


def fused(seq_count, dp_count, coarse, skip, skip_weight, depth_taps, cotangent):
    _, rows, channels = skip.shape
    shard = skip_weight.shape[0]
    chunks = channels // width
    chips = seq_count // 2
    half, wide = jnp.bfloat16, jnp.float32
    dma = pltpu.SemaphoreType.DMA
    extended = rows + 2 * halo
    results = pl.pallas_call(
        functools.partial(
            kernel, seq_count, dp_count, 1.0 / math.sqrt(rows * seq_count * dp_count)
        ),
        out_shape=(
            jax.ShapeDtypeStruct(coarse.shape, half),
            jax.ShapeDtypeStruct(skip.shape, half),
            jax.ShapeDtypeStruct(skip_weight.shape, wide),
            jax.ShapeDtypeStruct(depth_taps.shape, wide),
        ),
        in_specs=[pl.BlockSpec(memory_space=pltpu.HBM)] * 5,
        out_specs=(pl.BlockSpec(memory_space=pltpu.HBM),) * 4,
        scratch_shapes=[
            pltpu.VMEM(coarse.shape, half),
            pltpu.VMEM(skip.shape, half),
            pltpu.VMEM(skip_weight.shape, wide),
            pltpu.VMEM(depth_taps.shape, wide),
            pltpu.VMEM((extended, channels), half),
            pltpu.VMEM((extended, channels), half),
            pltpu.VMEM((rows // 2 + 2 * halo, channels), half),
            pltpu.VMEM((channels, rows), half),
            pltpu.VMEM((extended, rows // 2 + 2 * halo), half),
            pltpu.VMEM((rows // 2, rows), half),
            pltpu.VMEM((chunks, seq_count, shard, width), half),
            pltpu.VMEM((extended, width), wide),
            pltpu.VMEM((extended, width), wide),
            pltpu.VMEM((rows, channels), half),
            pltpu.VMEM((chunks, 2, chips, shard, width), wide),
            pltpu.VMEM((chunks, 2, chips, shard, width), half),
            pltpu.VMEM((chunks, chips, shard, width), half),
            pltpu.VMEM((chunks, chips, shard, width), half),
            pltpu.VMEM((chunks, shard, width), wide),
            pltpu.VMEM((chunks, chips - 1, shard, width), half),
            pltpu.VMEM((chunks, 4, shard // 2, 128), wide),
            pltpu.VMEM((chunks, 4, shard // 2, 128), half),
            pltpu.VMEM((chunks, dp_count - 1, shard // 2, 128), half),
            pltpu.VMEM((chunks, 4, shard // 2, 128), half),
            pltpu.VMEM(depth_taps.shape, wide),
            pltpu.VMEM((8, channels), wide),
            pltpu.VMEM((8, channels), wide),
            pltpu.VMEM((chips, 8, channels), wide),
            pltpu.VMEM((dp_count, 8, channels), wide),
            dma((8 + chunks,)),
            dma((6,)),
            dma((6,)),
            dma((chunks, chips - 1)),
            dma((chunks, chips - 1)),
            dma((chunks, chips - 1)),
            dma((chunks, chips - 1)),
            dma((chunks,)),
            dma((chunks,)),
            dma((chunks,)),
            dma((chunks,)),
            dma((chunks, chips - 1)),
            dma((chunks, chips - 1)),
            dma((chunks, dp_count - 1)),
            dma((chunks, dp_count - 1)),
            dma((chunks, dp_count - 1)),
            dma((chunks, dp_count - 1)),
            dma((chips + dp_count - 1,)),
            dma((chips + dp_count - 1,)),
        ],
        compiler_params=pltpu.CompilerParams(
            collective_id=0, has_side_effects=True, vmem_limit_bytes=62 * 1024 * 1024
        ),
    )(coarse, skip, skip_weight, depth_taps, cotangent)
    return pl.pallas_call(
        store,
        out_shape=tuple(jax.ShapeDtypeStruct(part.shape, part.dtype) for part in results),
        in_specs=[pl.BlockSpec(memory_space=pltpu.HBM)] * 4,
        out_specs=(pl.BlockSpec(memory_space=pltpu.HBM),) * 4,
        scratch_shapes=[pltpu.VMEM(part.shape, part.dtype) for part in results]
        + [dma((4,)), dma((4,))],
        compiler_params=pltpu.CompilerParams(vmem_limit_bytes=62 * 1024 * 1024),
    )(*results)


def solution(mesh):
    placed = (P("dp", "seq", None), P("dp", "seq", None), P("seq", None), P(), P("dp", "seq", None))
    seq_count, dp_count = mesh.shape["seq"], mesh.shape["dp"]

    def device_part(coarse, skip, skip_weight, depth_taps, cotangent):
        fits = (
            skip.shape[0] == 1
            and skip.shape[1] % tile == 0
            and skip.shape[2] % width == 0
            and skip_weight.shape[0] % 32 == 0
            and seq_count % 2 == 0
            and seq_count > 2
            and dp_count == 4
        )
        if fits:
            return fused(seq_count, dp_count, coarse, skip, skip_weight, depth_taps, cotangent)
        return local(coarse, skip, skip_weight, depth_taps, cotangent)

    return jax.shard_map(
        device_part,
        mesh=mesh,
        in_specs=placed,
        out_specs=(P("dp", "seq", None), P("dp", "seq", None), P("seq", None), P()),
        check_vma=False,
    )
```
